512 devices in a mesh: heads: 8 (over y), ctx: 64 (over z, x, core).
Axes of the slice: x: 4, y: 8, z: 8, core: 2. Of those that a mesh axis runs over, the one named last changes fastest.
Arguments:
- queries: bfloat16 [32, 16384, 128], P('heads', 'ctx'), may hold values from -6 to 6
- key_rows: bfloat16 [32, 16384, 128], P('heads', 'ctx'), may hold values from -6 to 6
- value_rows: bfloat16 [32, 16384, 128], P('heads', 'ctx'), may hold values from -6 to 6
- level_weights: float32 [32, 15, 16384], P('heads', None, 'ctx'), may hold values from 0.1 to 3
- norm_gain: float32 [32, 128], P('heads'), may hold values from 0.1 to 1.9
- grad_normed: bfloat16 [32, 16384, 128], P('heads', 'ctx'), may hold values from -6 to 6
Outputs:
- normed: bfloat16 [32, 16384, 128], P('heads', 'ctx')
- grad_queries: bfloat16 [32, 16384, 128], P('heads', 'ctx')
- grad_keys: bfloat16 [32, 16384, 128], P('heads', 'ctx')
- grad_values: bfloat16 [32, 16384, 128], P('heads', 'ctx')
- grad_level_weights: float32 [32, 15, 16384], P('heads', None, 'ctx')
The draws below stay inside these ranges and needn't reach their ends.
All inputs are finite; a program needn't handle non-finite values.
Results may differ from the reference program's by a relative error of at most 0.006.
Values sent between devices are 32-bit elements; how exact they have to be, the bound alone decides.
No kernel may reach another device: no remote copies, remote signals or barrier semaphores. Data moves between devices by JAX's collectives and lax.ppermute only.
A program may use at most 64 MiB of HBM per device.

```python
import math
import jax
import jax.numpy as jnp
from jax import lax

HD = 128
TOK_DEV = 256
HEADS = 32
TOKENS = 16384
LOCAL = 9
FAR = 6
LEVELS = 15
N_CTX = 64


def draw_level_weights(key, part):
    shape = (HEADS, LEVELS, TOKENS)
    head_pos = jnp.arange(HEADS, dtype=jnp.float32)
    rising = 1.0 + 2.0 * head_pos / max(HEADS - 1, 1)
    base = jnp.exp(jax.random.uniform(key, shape, jnp.float32, math.log(0.1), 0.0))
    return base * rising[:, None, None]


def block_levels(own_key, dims, pieces, least, high):
    factor_of = 1.0
    for dim, shards_of in pieces:
        steps = jax.random.uniform(jax.random.fold_in(jax.random.fold_in(own_key, 6), dim), (shards_of,), jnp.float32, least / len(pieces), high / len(pieces))
        factor_of = factor_of * jnp.repeat(jnp.exp(steps), dims[dim] // shards_of).reshape((-1,) + (1,) * (len(dims) - 1 - dim))
    return factor_of


def bell_draw(own_key, shape, deviation, reach, cuts=(), held_as=jnp.bfloat16):
    level = block_levels(own_key, shape, cuts, -0.22, 0.18) if cuts else 1.0
    result = jax.random.normal(own_key, shape, jnp.float32) * deviation * level
    return jnp.minimum(jnp.maximum(result, -reach), reach).astype(held_as)


def setup_inputs(seed: int = 0) -> dict:
    splits = jax.random.split(jax.random.key(seed), 7)
    queries = bell_draw(splits[0], (HEADS, TOKENS, HD), 1.0, 6.0, ((0, 8), (1, 64)))
    key_rows = bell_draw(splits[1], (HEADS, TOKENS, HD), 1.0, 6.0, ((0, 8), (1, 64)))
    value_rows = bell_draw(splits[2], (HEADS, TOKENS, HD), 1.0, 6.0, ((0, 8), (1, 64)))
    level_weights = draw_level_weights(jax.random.fold_in(splits[6], 71), 0)
    norm_gain = jnp.clip(1.0 + 0.18 * jax.random.normal(splits[4], (HEADS, HD), jnp.float32), 0.1, 1.9)
    grad_normed = bell_draw(splits[5], (HEADS, TOKENS, HD), 1.0, 6.0, ((0, 8), (1, 64)))
    return dict(queries=queries, key_rows=key_rows, value_rows=value_rows, level_weights=level_weights, norm_gain=norm_gain, grad_normed=grad_normed)


EPS = 1e-06
HIGH = lax.Precision.HIGHEST

def level_scale(number, head_dim):
    return 2.0 ** (-max(number - 1, 0) / 2.0) / math.sqrt(head_dim)

def level_matrix(count):
    position = jnp.arange(count, dtype=jnp.int32)
    differ = jnp.bitwise_xor(position[:, None], position[None, :])
    bucket = jnp.zeros((count, count), jnp.int32)
    for exponent in range(count.bit_length() - 1):
        bucket = bucket + (differ >= 2 ** exponent).astype(jnp.int32)
    causal = position[None, :] <= position[:, None]
    return (bucket, causal)

def near_weights(factors, bucket, causal, head_dim):
    weights = jnp.zeros(factors[0].shape + (bucket.shape[1],), jnp.float32)
    for number in range(len(factors)):
        scaled = factors[number] * level_scale(number, head_dim)
        weights = weights + jnp.where((bucket == number) & causal, scaled[..., None], jnp.float32(0.0))
    return weights

def far_states(key_value):
    stacked = []
    for depth in range(FAR):
        span = 2 ** depth
        group_sum = lax.optimization_barrier(jnp.sum(key_value.reshape(N_CTX // span, span, HD, HD), axis=1))
        before = jnp.concatenate([jnp.zeros((1, HD, HD), jnp.float32), group_sum[:-1]], 0)
        chosen = jnp.where((jnp.arange(N_CTX // span) % 2 == 1)[:, None, None], before, jnp.float32(0.0))
        stacked.append(jnp.repeat(chosen, span, axis=0))
    return jnp.stack(stacked, 0)

def back_states(grad_states):
    total = jnp.zeros((N_CTX, HD, HD), jnp.float32)
    for depth in range(FAR):
        span = 2 ** depth
        group_sum = lax.optimization_barrier(jnp.sum(grad_states[depth].reshape(N_CTX // span, span, HD, HD), axis=1))
        after = jnp.concatenate([group_sum[1:], jnp.zeros((1, HD, HD), jnp.float32)], 0)
        chosen = jnp.where((jnp.arange(N_CTX // span) % 2 == 0)[:, None, None], after, jnp.float32(0.0))
        total = total + jnp.repeat(chosen, span, axis=0)
    return total

def prepare(packed):
    query_head, key_head, value_head, rate_head = packed[:4]
    q_blocks = query_head.reshape(N_CTX, TOK_DEV, HD).astype(jnp.float32)
    k_blocks = key_head.reshape(N_CTX, TOK_DEV, HD).astype(jnp.float32)
    v_blocks = value_head.reshape(N_CTX, TOK_DEV, HD).astype(jnp.float32)
    rate_blocks = rate_head.reshape(LEVELS, N_CTX, TOK_DEV)
    key_value = jnp.einsum('nsd,nse->nde', k_blocks, v_blocks, precision=HIGH)
    states = far_states(key_value)
    bucket, causal = level_matrix(TOK_DEV)
    weights = near_weights([rate_blocks[number] for number in range(LOCAL)], bucket, causal, HD)
    scores = jnp.einsum('ntd,nsd->nts', q_blocks, k_blocks, precision=HIGH)
    weighted = lax.optimization_barrier((weights * scores).astype(jnp.bfloat16)).astype(jnp.float32)
    far_scale = jnp.stack([rate_blocks[LOCAL + depth] * level_scale(LOCAL + depth, HD) for depth in range(FAR)], 0)
    far_terms = jnp.einsum('ntd,mnde->mnte', q_blocks, states, precision=HIGH)
    return (q_blocks, k_blocks, v_blocks, states, bucket, causal, weights, scores, weighted, far_scale, far_terms)

def forward_head(packed):
    q_blocks, k_blocks, v_blocks, states, bucket, causal, weights, scores, weighted, far_scale, far_terms = prepare(packed)
    near_out = jnp.einsum('nts,nse->nte', weighted, v_blocks, precision=HIGH)
    attended = near_out + lax.optimization_barrier(jnp.sum(far_scale[..., None] * far_terms, 0))
    return attended.reshape(TOKENS, HD)

def backward_head(packed):
    q_blocks, k_blocks, v_blocks, states, bucket, causal, weights, scores, weighted, far_scale, far_terms = prepare(packed)
    grad_out = packed[4].reshape(N_CTX, TOK_DEV, HD).astype(jnp.float32)
    grad_mix = jnp.einsum('nte,nse->nts', grad_out, v_blocks, precision=HIGH)
    product = grad_mix * scores
    near_grads = [level_scale(number, HD) * lax.optimization_barrier(jnp.sum(jnp.where((bucket == number) & causal, product, jnp.float32(0.0)), axis=2)) for number in range(LOCAL)]
    far_grads = [level_scale(LOCAL + depth, HD) * lax.optimization_barrier(jnp.sum(grad_out * far_terms[depth], axis=2)) for depth in range(FAR)]
    grad_scores = lax.optimization_barrier((weights * grad_mix).astype(jnp.bfloat16)).astype(jnp.float32)
    grad_q = jnp.einsum('nts,nsd->ntd', grad_scores, k_blocks, precision=HIGH)
    grad_q = grad_q + lax.optimization_barrier(jnp.sum(far_scale[..., None] * jnp.einsum('nte,mnde->mntd', grad_out, states, precision=HIGH), 0))
    scaled_queries = lax.optimization_barrier((far_scale[..., None] * q_blocks[None]).astype(jnp.bfloat16)).astype(jnp.float32)
    grad_states = jnp.einsum('mntd,nte->mnde', scaled_queries, grad_out, precision=HIGH)
    grad_kv = lax.optimization_barrier(back_states(grad_states).astype(jnp.bfloat16)).astype(jnp.float32)
    grad_k = jnp.einsum('nts,ntd->nsd', grad_scores, q_blocks, precision=HIGH) + jnp.einsum('nse,nde->nsd', v_blocks, grad_kv, precision=HIGH)
    grad_v = jnp.einsum('nts,nte->nse', weighted, grad_out, precision=HIGH) + jnp.einsum('nsd,nde->nse', k_blocks, grad_kv, precision=HIGH)
    grad_rates = jnp.stack(near_grads + far_grads, 0).reshape(LEVELS, TOKENS)
    return (grad_q.reshape(TOKENS, HD).astype(jnp.bfloat16), grad_k.reshape(TOKENS, HD).astype(jnp.bfloat16), grad_v.reshape(TOKENS, HD).astype(jnp.bfloat16), grad_rates)

def reference(queries, key_rows, value_rows, level_weights, norm_gain, grad_normed):
    attended = lax.map(forward_head, (queries, key_rows, value_rows, level_weights))
    width = HEADS * HD
    totals = lax.optimization_barrier(jnp.sum(attended * attended, axis=(0, 2)))
    inv_rms = lax.rsqrt(totals / width + EPS)
    normed = (attended * inv_rms[None, :, None] * norm_gain[:, None, :]).astype(jnp.bfloat16)
    scaled = norm_gain[:, None, :] * grad_normed.astype(jnp.float32)
    inner_sum = lax.optimization_barrier(jnp.sum(scaled * attended, axis=(0, 2)))
    grad_out = (inv_rms[None, :, None] * scaled - attended * (inv_rms ** 3 * inner_sum / width)[None, :, None]).astype(jnp.bfloat16)
    grad_q, grad_k, grad_v, grad_rates = lax.map(backward_head, (queries, key_rows, value_rows, level_weights, grad_out))
    return (normed, grad_q, grad_k, grad_v, grad_rates)
```

```python
import math

import jax
import jax.numpy as jnp
from jax import lax
from jax.experimental import pallas as pl
from jax.experimental.pallas import tpu as pltpu
from jax.sharding import Mesh
from jax.sharding import PartitionSpec as P

EPS = 1e-06
HIGH = lax.Precision.HIGHEST
F32 = jnp.float32
BF16 = jnp.bfloat16

NH = 4
TOK = 256
HD = 128
LOCAL = 9
FAR = 6
PLANE = 3
WIDTH = 32 * HD
MIB = 2**20

CTX = ("z", "x", "core")
ROWS = ("z", "x")
FLAT = ("x", "core")


def level_scale(number):
    return 2.0 ** (-max(number - 1, 0) / 2.0) / math.sqrt(HD)


def dot(a, b, ca, cb, precision=None):
    return lax.dot_general(
        a, b, (((ca,), (cb,)), ((), ())), precision=precision, preferred_element_type=F32
    )


def call(body, outs, operands, flops, moved, limit=32):
    vmem = pl.BlockSpec(memory_space=pltpu.VMEM)
    return pl.pallas_call(
        body,
        out_shape=[jax.ShapeDtypeStruct(s, d) for s, d in outs],
        in_specs=[vmem] * len(operands),
        out_specs=[vmem] * len(outs),
        cost_estimate=pl.CostEstimate(flops=flops, bytes_accessed=moved, transcendentals=0),
        compiler_params=pltpu.CompilerParams(vmem_limit_bytes=limit * MIB),
    )(*operands)


def key_value_body(k_ref, v_ref, kv_ref):
    for h in range(NH):
        kv_ref[h] = dot(k_ref[h], v_ref[h], 0, 0)


def level_masks():
    s = lax.broadcasted_iota(jnp.int32, (TOK, TOK), 0)
    t = lax.broadcasted_iota(jnp.int32, (TOK, TOK), 1)
    differ = s ^ t
    bucket = jnp.zeros((TOK, TOK), jnp.int32)
    for exponent in range(LOCAL - 1):
        bucket = bucket + (differ >= 2**exponent).astype(jnp.int32)
    return jnp.where(s <= t, bucket, -1)


def near_body(q_ref, k_ref, v_ref, lw_ref, sc_ref, wt_ref, wd_ref, no_ref, sq_ref, sqt_ref):
    level = level_masks()
    for h in range(NH):
        q, k, v = q_ref[h], k_ref[h], v_ref[h]
        lw = lw_ref[h]
        scores = dot(k, q, 1, 1)
        weights = jnp.zeros((TOK, TOK), F32)
        for number in range(LOCAL):
            row = lw[number : number + 1, :] * level_scale(number)
            weights = jnp.where(level == number, row, weights)
        weighted = (weights * scores).astype(BF16)
        sc_ref[h] = scores
        wt_ref[h] = weights
        wd_ref[h] = weighted
        no_ref[h] = dot(weighted, v, 0, 0)
        q_t = q.astype(F32).T
        for m in range(FAR):
            row = lw[LOCAL + m : LOCAL + m + 1, :] * level_scale(LOCAL + m)
            scaled_t = (q_t * row).astype(BF16)
            sqt_ref[h, m * HD : (m + 1) * HD, :] = scaled_t
            sq_ref[h, :, m * HD : (m + 1) * HD] = scaled_t.astype(F32).T.astype(BF16)


def plane_body(gath_ref, sq_ref, no_ref, part_ref, st_ref):
    p = lax.axis_index("x") * 2 + lax.axis_index("core")
    zero = jnp.float32(0.0)
    for h in range(NH):
        one = gath_ref[jnp.maximum(p - 1, 0), h]
        s0 = jnp.where((p & 1) == 1, one, zero)
        base = jnp.maximum((p >> 1) * 2 - 2, 0)
        s1 = jnp.where((p & 2) == 2, gath_ref[base, h] + gath_ref[base + 1, h], zero)
        four = (gath_ref[0, h] + gath_ref[1, h]) + (gath_ref[2, h] + gath_ref[3, h])
        s2 = jnp.where((p & 4) == 4, four, zero)
        states = jnp.concatenate([s0, s1, s2], axis=0).astype(BF16)
        st_ref[h] = states
        part_ref[h] = no_ref[h] + dot(sq_ref[h, :, : PLANE * HD], states, 1, 0)


def owner_forward_body(in_ref, out_ref):
    sums = []
    for z in range(8):
        total = in_ref[8 * z]
        for p in range(1, 8):
            total = total + in_ref[8 * z + p]
        sums.append(total)
    nothing = jnp.zeros((8, HD), F32)
    pair0 = sums[0] + sums[1]
    pair2 = sums[4] + sums[5]
    four = pair0 + (sums[2] + sums[3])
    for z in range(8):
        first = sums[z - 1] if z & 1 else nothing
        second = (pair2 if z & 4 else pair0) if z & 2 else nothing
        third = four if z & 4 else nothing
        for x in range(4):
            out_ref[4 * z + x, 0] = first
            out_ref[4 * z + x, 1] = second
            out_ref[4 * z + x, 2] = third


def attend_body(pc_ref, part_ref, sq_ref, gn_ref, gain_ref, att_ref, st_ref, pay_ref):
    squares = jnp.zeros((TOK, HD), F32)
    inner = jnp.zeros((TOK, HD), F32)
    for h in range(NH):
        states = []
        for m in range(PLANE):
            tiles = []
            for i in range(16):
                tiles.append(pc_ref[i % 2, 8 * h + i // 2, m])
            states.append(jnp.concatenate(tiles, axis=0))
        states = jnp.concatenate(states, axis=0).astype(BF16)
        st_ref[h] = states
        att = part_ref[h] + dot(sq_ref[h, :, PLANE * HD :], states, 1, 0)
        att_ref[h] = att
        scaled = gain_ref[h : h + 1, :] * gn_ref[h].astype(F32)
        squares = squares + att * att
        inner = inner + scaled * att
    ones = jnp.ones((8, HD), F32)
    squares_row = dot(ones, squares, 1, 1, HIGH)
    inner_row = dot(ones, inner, 1, 1, HIGH)
    half = TOK // 2
    tile = jnp.concatenate(
        [
            squares_row[0:1, :half],
            squares_row[0:1, half:],
            inner_row[0:1, :half],
            inner_row[0:1, half:],
            jnp.zeros((4, HD), F32),
        ],
        axis=0,
    )
    for peer in range(8):
        pay_ref[peer] = tile


def token_columns(recv_ref):
    total = recv_ref[0]
    for peer in range(1, 8):
        total = total + recv_ref[peer]
    inv = lax.rsqrt(total[0:2] / WIDTH + EPS)
    coef = inv * inv * inv * total[2:4] / WIDTH
    table = jnp.concatenate([inv, coef, jnp.zeros((4, HD), F32)], axis=0).T
    inv_col = jnp.concatenate([table[:, 0:1], table[:, 1:2]], axis=0)
    coef_col = jnp.concatenate([table[:, 2:3], table[:, 3:4]], axis=0)
    return inv_col, coef_col


def grad_body(recv_ref, att_ref, gn_ref, gain_ref, sqt_ref, go_ref, own_ref, send_ref, flat_ref):
    core = lax.axis_index("core")
    p = lax.axis_index("x") * 2 + core
    inv_col, coef_col = token_columns(recv_ref)
    zero = jnp.float32(0.0)
    for h in range(NH):
        scaled = gain_ref[h : h + 1, :] * gn_ref[h].astype(F32)
        go = (inv_col * scaled - att_ref[h] * coef_col).astype(BF16)
        go_ref[h] = go
        states = dot(sqt_ref[h], go, 1, 0)
        for m in range(PLANE):
            for k in range(8):
                row = (PLANE + m) * HD + 16 * k
                even = states[row : row + 8]
                odd = states[row + 8 : row + 16]
                own_ref[8 * h + k, m] = jnp.where(core == 0, even, odd)
                send_ref[8 * h + k, m] = jnp.where(core == 0, odd, even)
        for peer in range(8):
            value = jnp.zeros((HD, HD), F32)
            for m in range(PLANE):
                if not (peer >> m) & 1:
                    chosen = (p >> m) == (peer >> m) + 1
                    value = jnp.where(chosen, states[m * HD : (m + 1) * HD], value)
            flat_ref[peer, h] = value


def pair_body(own_ref, gath_ref, out_ref):
    other = 1 - lax.axis_index("core")
    out_ref[...] = own_ref[...] + gath_ref[other]


def owner_backward_body(in_ref, out_ref):
    grads = []
    for m in range(PLANE):
        rows = []
        for z in range(8):
            total = in_ref[4 * z, m]
            for x in range(1, 4):
                total = total + in_ref[4 * z + x, m]
            rows.append(total)
        grads.append(rows)
    pair2 = grads[1][2] + grads[1][3]
    pair6 = grads[1][6] + grads[1][7]
    four = (grads[2][4] + grads[2][5]) + (grads[2][6] + grads[2][7])
    for z in range(8):
        total = jnp.zeros((8, HD), F32)
        if not z & 1:
            total = total + grads[0][z + 1]
        if not z & 2:
            total = total + (pair6 if z & 4 else pair2)
        if not z & 4:
            total = total + four
        for p in range(8):
            out_ref[8 * z + p] = total


def back_body(
    q_ref, k_ref, v_ref, lw_ref, go_ref, att_ref, gain_ref, recv_ref, sc_ref, wt_ref, wd_ref,
    low_ref, high_ref, nm_ref, gq_ref, gk_ref, gv_ref, gl_ref,
):
    level = level_masks()
    inv_col, _ = token_columns(recv_ref)
    for h in range(NH):
        q, k, v, go = q_ref[h], k_ref[h], v_ref[h], go_ref[h]
        lw = lw_ref[h]
        nm_ref[h] = (att_ref[h] * inv_col * gain_ref[h : h + 1, :]).astype(BF16)
        mix = dot(v, go, 1, 1)
        product = mix * sc_ref[h]
        rows = []
        for number in range(LOCAL):
            picked = jnp.where(level == number, product, jnp.float32(0.0))
            rows.append(level_scale(number) * jnp.sum(picked, axis=0, keepdims=True))
        grad_scores = (wt_ref[h] * mix).astype(BF16)
        gk_ref[h] = dot(grad_scores, q, 1, 0)
        gv_ref[h] = dot(wd_ref[h], go, 1, 0)
        q_t = q.astype(F32).T
        far_t = jnp.zeros((HD, TOK), F32)
        for part, states_ref in enumerate((low_ref, high_ref)):
            turned = dot(states_ref[h], go, 1, 1)
            for m in range(PLANE):
                piece = turned[m * HD : (m + 1) * HD]
                number = LOCAL + part * PLANE + m
                row = lw[number : number + 1, :] * level_scale(number)
                far_t = far_t + row * piece
                rows.append(level_scale(number) * jnp.sum(piece * q_t, axis=0, keepdims=True))
        gq_ref[h] = (dot(grad_scores, k, 0, 0) + far_t.T).astype(BF16)
        gl_ref[h] = jnp.concatenate(rows, axis=0)


def final_body(piece_ref, flat_ref, k_ref, v_ref, gk_ref, gv_ref, outk_ref, outv_ref):
    for h in range(NH):
        grad_kv = (piece_ref[h] + flat_ref[h]).astype(BF16)
        outk_ref[h] = (gk_ref[h] + dot(v_ref[h], grad_kv, 1, 1)).astype(BF16)
        outv_ref[h] = (gv_ref[h] + dot(k_ref[h], grad_kv, 1, 0)).astype(BF16)


def swap(value, axes):
    return lax.all_to_all(value, axes, split_axis=0, concat_axis=0, tiled=True)


def shards(queries, key_rows, value_rows, level_weights, norm_gain, grad_normed):
    tokens = (NH, TOK, HD)
    square = (NH, TOK, TOK)
    matrix = (NH, HD, HD)
    stacked = (NH, PLANE * HD, HD)
    pieces = (32, PLANE, 8, HD)

    (kv,) = call(key_value_body, [(matrix, F32)], (key_rows, value_rows), 2**25, MIB)
    gathered = lax.all_gather(kv, FLAT, axis=0, tiled=False)
    owned = swap(kv.reshape(64, 8, HD), CTX)
    scores, weights, weighted, near_out, sq, sqt = call(
        near_body,
        [
            (square, F32),
            (square, F32),
            (square, BF16),
            (tokens, F32),
            ((NH, TOK, FAR * HD), BF16),
            ((NH, FAR * HD, TOK), BF16),
        ],
        (queries, key_rows, value_rows, level_weights),
        2**27,
        8 * MIB,
    )
    (outgoing,) = call(owner_forward_body, [(pieces, F32)], (owned,), 2**17, MIB // 2)
    arrived = swap(outgoing, ROWS)
    part, low = call(
        plane_body, [(tokens, F32), (stacked, BF16)], (gathered, sq, near_out), 2**27, 5 * MIB
    )
    both = lax.all_gather(arrived, "core", axis=0, tiled=False)
    attended, high, payload = call(
        attend_body,
        [(tokens, F32), (stacked, BF16), ((8, 8, HD), F32)],
        (both, part, sq, grad_normed, norm_gain),
        2**27,
        4 * MIB,
    )
    sums = swap(payload, "heads")
    grad_out, own, send, flat = call(
        grad_body,
        [(tokens, BF16), (pieces, F32), (pieces, F32), ((8,) + matrix, F32)],
        (sums, attended, grad_normed, norm_gain, sqt),
        2**28,
        6 * MIB,
    )
    flat_sum = lax.psum_scatter(flat, FLAT, scatter_dimension=0, tiled=False)
    sibling = lax.all_gather(send, "core", axis=0, tiled=False)
    (joined,) = call(pair_body, [(pieces, F32)], (own, sibling), 2**17, 3 * MIB // 2)
    returned = swap(joined, ROWS)
    normed, grad_q, near_k, near_v, grad_rates = call(
        back_body,
        [
            (tokens, BF16),
            (tokens, BF16),
            (tokens, F32),
            (tokens, F32),
            ((NH, LOCAL + FAR, TOK), F32),
        ],
        (
            queries, key_rows, value_rows, level_weights, grad_out, attended, norm_gain, sums,
            scores, weights, weighted, low, high,
        ),
        2**28,
        8 * MIB,
    )
    (spread,) = call(owner_backward_body, [((64, 8, HD), F32)], (returned,), 2**17, MIB // 2)
    total = swap(spread, CTX).reshape(matrix)
    grad_k, grad_v = call(
        final_body,
        [(tokens, BF16), (tokens, BF16)],
        (total, flat_sum, key_rows, value_rows, near_k, near_v),
        2**26,
        3 * MIB,
    )
    return normed, grad_q, grad_k, grad_v, grad_rates


def solution(mesh):
    grid = Mesh(mesh.devices.reshape(8, 8, 4, 2), ("heads",) + CTX)
    rows = P("heads", CTX, None)
    rates = P("heads", None, CTX)
    return jax.shard_map(
        shards,
        mesh=grid,
        in_specs=(rows, rows, rows, rates, P("heads", None), rows),
        out_specs=(rows, rows, rows, rows, rates),
        check_vma=False,
    )
```

```python
import math

import jax
import jax.numpy as jnp
from jax import lax
from jax.experimental import pallas as pl
from jax.experimental.pallas import tpu as pltpu
from jax.sharding import Mesh
from jax.sharding import PartitionSpec as P

EPS = 1e-06
F32 = jnp.float32
BF16 = jnp.bfloat16

NH = 4
TOK = 256
HD = 128
LOCAL = 9
FAR = 6
PLANE = 3
WIDTH = 32 * HD
MIB = 2**20
ALONE = 60

CTX = ("z", "x", "core")
ROWS = ("z", "x")

TOKENS = (NH, TOK, HD)
TURNED = (NH, HD, TOK)
MATRIX = (NH, HD, HD)
HALF = (NH // 2, HD, HD)
STACKED = (NH, PLANE * HD, HD)
PIECES = (32, PLANE, 8, HD)


def level_scale(number):
    return 2.0 ** (-max(number - 1, 0) / 2.0) / math.sqrt(HD)


def dot(a, b, ca, cb):
    return lax.dot_general(a, b, (((ca,), (cb,)), ((), ())), preferred_element_type=F32)


def call(body, outs, operands, flops, moved, far_in=(), far_out=(), limit=16, after=(), views={}):
    near = pl.BlockSpec(memory_space=pltpu.VMEM)
    far = pl.BlockSpec(memory_space=pltpu.HBM)
    count = len(operands)
    shapes = [views[i][0] if i in views else a.shape for i, a in enumerate(operands)]
    buffers = [pltpu.VMEM(shapes[i], operands[i].dtype) for i in far_in]
    buffers += [pltpu.VMEM(*outs[i]) for i in far_out]

    def split(shape):
        return shape[0] == NH and len(shape) > 2

    parts = [NH if split(shapes[i]) else 1 for i in far_in]
    parts += [NH if split(outs[i][0]) else 1 for i in far_out]
    copies = sum(parts)

    def wrapped(*refs):
        refs = list(refs)
        sems = refs.pop() if copies else None
        del refs[count : count + len(after)]
        scratch = refs[count + len(outs) :]
        used = refs[: count + len(outs)]
        whole, before, behind, last = [], [[] for _ in range(NH)], [[] for _ in range(NH)], []
        sem = 0
        for slot, i in enumerate(far_in):
            held = scratch[slot]
            if i in views:
                used[i] = views[i][1](used[i])
            if parts[slot] == NH:
                for h in range(NH):
                    before[h].append(
                        pltpu.make_async_copy(used[i].at[h], held.at[h], sems.at[sem + h])
                    )
            else:
                whole.append(pltpu.make_async_copy(used[i], held, sems.at[sem]))
            sem += parts[slot]
            used[i] = held
        for slot, i in enumerate(far_out, len(far_in)):
            held = scratch[slot]
            if parts[slot] == NH:
                for h in range(NH):
                    behind[h].append(
                        pltpu.make_async_copy(held.at[h], used[count + i].at[h], sems.at[sem + h])
                    )
            else:
                last.append(pltpu.make_async_copy(held, used[count + i], sems.at[sem]))
            sem += parts[slot]
            used[count + i] = held
        for copy in whole + sum(before, []):
            copy.start()
        for copy in whole:
            copy.wait()
        step = body(*used)
        for h in range(NH):
            for copy in before[h]:
                copy.wait()
            if step is not None:
                step(h)
            for copy in behind[h]:
                copy.start()
        for copy in last:
            copy.start()
        for copy in sum(behind, []) + last:
            copy.wait()

    return pl.pallas_call(
        wrapped,
        out_shape=[jax.ShapeDtypeStruct(s, d) for s, d in outs],
        in_specs=[far if i in far_in else near for i in range(count)]
        + [pl.BlockSpec(memory_space=pl.ANY)] * len(after),
        out_specs=[far if i in far_out else near for i in range(len(outs))],
        scratch_shapes=buffers + ([pltpu.SemaphoreType.DMA((copies,))] if copies else []),
        cost_estimate=pl.CostEstimate(flops=flops, bytes_accessed=moved, transcendentals=0),
        compiler_params=pltpu.CompilerParams(vmem_limit_bytes=int(limit * MIB)),
    )(*operands, *after)


def key_value_body(k_ref, v_ref, kv_ref):
    def step(h):
        kv_ref[h] = dot(k_ref[h], v_ref[h], 0, 0)

    return step


def level_masks():
    s = lax.broadcasted_iota(jnp.int32, (TOK, TOK), 0)
    t = lax.broadcasted_iota(jnp.int32, (TOK, TOK), 1)
    differ = s ^ t
    bucket = jnp.zeros((TOK, TOK), jnp.int32)
    for exponent in range(LOCAL - 1):
        bucket = bucket + (differ >= 2**exponent).astype(jnp.int32)
    return jnp.where(s <= t, bucket, -1)


def level_row(lw_ref, number, h):
    return lw_ref[number, h : h + 1, :] * level_scale(number)


def near_weights(lw_ref, level, h):
    weights = jnp.zeros((TOK, TOK), F32)
    for number in range(LOCAL):
        weights = jnp.where(level == number, level_row(lw_ref, number, h), weights)
    return weights


def scaled_queries(q_t, lw_ref, part, h):
    levels = [LOCAL + part * PLANE + m for m in range(PLANE)]
    return jnp.concatenate([q_t * level_row(lw_ref, n, h) for n in levels], axis=0).astype(BF16)


def near_body(
    lw_ref, gain_ref, wide_ref, both_ref, q_ref, k_ref, v_ref, gn_ref, mixed_ref, st_ref, qt_ref
):
    level = level_masks()
    odd = lax.axis_index("core") == 1

    def step(h):
        q = q_ref[h]
        scores = dot(k_ref[h], q, 1, 1)
        weighted = (near_weights(lw_ref, level, h) * scores).astype(BF16)
        q_t = q.astype(F32).T
        qt_ref[h] = q_t.astype(BF16)
        s0 = jnp.where(odd, both_ref[h], jnp.float32(0.0))
        s1 = wide_ref[h // 2, 0, h % 2]
        s2 = wide_ref[h // 2, 1, h % 2]
        states = jnp.concatenate([s0, s1, s2], axis=0).astype(BF16)
        st_ref[h] = states
        far = dot(states, scaled_queries(q_t, lw_ref, 0, h), 0, 0)
        mixed_ref[h, 0] = dot(v_ref[h], weighted, 0, 0) + far
        mixed_ref[h, 1] = (gain_ref[h : h + 1, :] * gn_ref[h].astype(F32)).T

    return step


def half_body(both_ref, out_ref):
    first = lax.axis_index("core") * (NH // 2)
    for h in range(NH // 2):
        out_ref[h] = both_ref[0, first + h] + both_ref[1, first + h]


def collect_body(step1_ref, step2_ref, out_ref):
    odd = (lax.axis_index("x") & 1) == 1
    for h in range(NH // 2):
        out_ref[0, h] = jnp.where(odd, step1_ref[h], jnp.float32(0.0))
        out_ref[1, h] = step2_ref[h]


def add_body(a_ref, b_ref, out_ref):
    out_ref[...] = a_ref[...] + b_ref[...]


def add_odd_body(a_ref, b_ref, out_ref):
    odd = (lax.axis_index("x") & 1) == 1
    out_ref[...] = jnp.where(odd, a_ref[...], jnp.float32(0.0)) + b_ref[...]


def owner_forward_body(in_ref, out_ref):
    sums = []
    for z in range(8):
        total = in_ref[8 * z]
        for p in range(1, 8):
            total = total + in_ref[8 * z + p]
        sums.append(total)
    nothing = jnp.zeros((8, HD), F32)
    pair0 = sums[0] + sums[1]
    pair2 = sums[4] + sums[5]
    four = pair0 + (sums[2] + sums[3])
    for z in range(8):
        first = sums[z - 1] if z & 1 else nothing
        second = (pair2 if z & 4 else pair0) if z & 2 else nothing
        third = four if z & 4 else nothing
        for x in range(4):
            out_ref[4 * z + x, 0] = first
            out_ref[4 * z + x, 1] = second
            out_ref[4 * z + x, 2] = third


def attend_body(pc_ref, lw_ref, mixed_ref, qt_ref, att_ref, st_ref, pay_ref):
    squares = jnp.zeros((HD, TOK), F32)
    inner = jnp.zeros((HD, TOK), F32)
    for h in range(NH):
        tiles = []
        for m in range(PLANE):
            for i in range(16):
                tiles.append(pc_ref[i % 2, 8 * h + i // 2, m])
        states = jnp.concatenate(tiles, axis=0).astype(BF16)
        st_ref[h] = states
        sq = scaled_queries(qt_ref[h].astype(F32), lw_ref, 1, h)
        att = mixed_ref[h, 0] + dot(states, sq, 0, 0)
        att_ref[h] = att
        squares = squares + att * att
        inner = inner + mixed_ref[h, 1] * att
    squares = jnp.sum(squares, axis=0, keepdims=True)
    inner = jnp.sum(inner, axis=0, keepdims=True)
    rows = [squares[:, :HD], squares[:, HD:], inner[:, :HD], inner[:, HD:]]
    tile = jnp.concatenate(rows + [jnp.zeros((4, HD), F32)], axis=0)
    for peer in range(8):
        pay_ref[peer] = tile


def token_rows(recv_ref):
    total = recv_ref[0]
    for peer in range(1, 8):
        total = total + recv_ref[peer]
    inv = lax.rsqrt(total[0:2] / WIDTH + EPS)
    coef = inv * inv * inv * total[2:4] / WIDTH
    inv_row = jnp.concatenate([inv[0:1], inv[1:2]], axis=1)
    coef_row = jnp.concatenate([coef[0:1], coef[1:2]], axis=1)
    return inv_row, coef_row


def grad_body(
    recv_ref, lw_ref, att_ref, mixed_ref, qt_ref, own_ref, send_ref, keep_ref, give_ref
):
    first = lax.axis_index("core") == 0
    inv_row, coef_row = token_rows(recv_ref)
    for h in range(NH):
        go = (inv_row * mixed_ref[h, 1] - att_ref[h] * coef_row).astype(BF16)
        q_t = qt_ref[h].astype(F32)
        states = dot(scaled_queries(q_t, lw_ref, 1, h), go, 1, 1)
        for m in range(PLANE):
            for k in range(8):
                row = m * HD + 16 * k
                even = states[row : row + 8]
                odd = states[row + 8 : row + 16]
                own_ref[8 * h + k, m] = jnp.where(first, even, odd)
                send_ref[8 * h + k, m] = jnp.where(first, odd, even)
        states = dot(scaled_queries(q_t, lw_ref, 0, h), go, 1, 1)
        mine = first if h < NH // 2 else jnp.logical_not(first)
        for m in range(PLANE):
            value = states[m * HD : (m + 1) * HD]

            @pl.when(mine)
            def _keep(value=value, m=m, h=h):
                keep_ref[m, h % 2] = value

            @pl.when(jnp.logical_not(mine))
            def _give(value=value, m=m, h=h):
                give_ref[m, h % 2] = value


def pair_body(own_ref, gath_ref, out_ref):
    other = 1 - lax.axis_index("core")
    out_ref[...] = own_ref[...] + gath_ref[other]


def join_body(keep_ref, gath_ref, first_ref, second_ref):
    other = 1 - lax.axis_index("core")
    for h in range(NH // 2):
        first_ref[h] = keep_ref[1, h] + gath_ref[other, 1, h]
        second_ref[h] = keep_ref[2, h] + gath_ref[other, 2, h]


def merge_body(back1_ref, back2_ref, keep_ref, gath_ref, mine_ref, send_ref):
    first = lax.axis_index("core") == 0
    zero = jnp.float32(0.0)
    for h in range(NH // 2):
        total = back1_ref[h] + back2_ref[h]
        mine_ref[h] = total + jnp.where(first, gath_ref[1, 0, h], zero)
        send_ref[h] = total + jnp.where(first, zero, keep_ref[0, h])


def owner_backward_body(in_ref, out_ref):
    grads = []
    for m in range(PLANE):
        rows = []
        for z in range(8):
            total = in_ref[4 * z, m]
            for x in range(1, 4):
                total = total + in_ref[4 * z + x, m]
            rows.append(total)
        grads.append(rows)
    pair2 = grads[1][2] + grads[1][3]
    pair6 = grads[1][6] + grads[1][7]
    four = (grads[2][4] + grads[2][5]) + (grads[2][6] + grads[2][7])
    for z in range(8):
        total = jnp.zeros((8, HD), F32)
        if not z & 1:
            total = total + grads[0][z + 1]
        if not z & 2:
            total = total + (pair6 if z & 4 else pair2)
        if not z & 4:
            total = total + four
        for p in range(8):
            out_ref[8 * z + p] = total


def back_body(
    recv_ref, gain_ref, lw_ref, q_ref, k_ref, v_ref, mixed_ref, att_ref, low_ref, high_ref,
    nm_ref, gq_ref, gk_ref, gv_ref, gl_ref,
):
    level = level_masks()
    inv_row, coef_row = token_rows(recv_ref)

    def step(h):
        q, k, att = q_ref[h], k_ref[h], att_ref[h]
        go = (inv_row * mixed_ref[h] - att * coef_row).astype(BF16)
        nm_ref[h] = ((att * inv_row).T * gain_ref[h : h + 1, :]).astype(BF16)
        scores = dot(k, q, 1, 1)
        weights = near_weights(lw_ref, level, h)
        mix = dot(v_ref[h], go, 1, 0)
        gv_ref[h] = dot((weights * scores).astype(BF16), go, 1, 1)
        grad_scores = (weights * mix).astype(BF16)
        gk_ref[h] = dot(grad_scores, q, 1, 0)
        product = mix * scores
        rows = []
        for number in range(LOCAL):
            picked = jnp.where(level == number, product, jnp.float32(0.0))
            rows.append(level_scale(number) * jnp.sum(picked, axis=0, keepdims=True))
        q_t = q.astype(F32).T
        far_t = dot(k, grad_scores, 0, 0)
        for part, states_ref in enumerate((low_ref, high_ref)):
            turned = dot(states_ref[h], go, 1, 0)
            for m in range(PLANE):
                piece = turned[m * HD : (m + 1) * HD]
                number = LOCAL + part * PLANE + m
                far_t = far_t + level_row(lw_ref, number, h) * piece
                rows.append(level_scale(number) * jnp.sum(piece * q_t, axis=0, keepdims=True))
        gq_ref[h] = far_t.T.astype(BF16)
        for number in range(LOCAL + FAR):
            gl_ref[number, h : h + 1, :] = rows[number]

    return step


def final_body(piece_ref, mine_ref, wide_ref, k_ref, v_ref, gk_ref, gv_ref, outk_ref, outv_ref):
    first = lax.axis_index("core") == 0

    def step(h):
        mine = first if h < NH // 2 else jnp.logical_not(first)
        plane = jnp.where(mine, mine_ref[h % 2], wide_ref[h // 2, h % 2])
        grad_kv = (piece_ref[h] + plane).astype(BF16)
        outk_ref[h] = (gk_ref[h] + dot(v_ref[h], grad_kv, 1, 1)).astype(BF16)
        outv_ref[h] = (gv_ref[h] + dot(k_ref[h], grad_kv, 1, 0)).astype(BF16)

    return step


def swap(value, axes):
    return lax.all_to_all(value, axes, split_axis=0, concat_axis=0, tiled=True)


def both_cores(value):
    return lax.all_gather(value, "core", axis=0, tiled=False)


def shards(queries, key_rows, value_rows, level_weights, norm_gain, grad_normed):
    rates = jnp.transpose(level_weights, (1, 0, 2))
    (kv,) = call(
        key_value_body, [(MATRIX, F32)], (key_rows, value_rows), 2**25, MIB, (0, 1), (), ALONE
    )
    owned = swap(kv.reshape(64, 8, HD), CTX)
    both = both_cores(kv)
    (pair,) = call(half_body, [(HALF, F32)], (both,), 2**16, MIB)
    step1 = lax.ppermute(pair, "x", [(0, 1), (1, 0), (2, 3), (3, 2)])
    owned, step1 = lax.optimization_barrier((owned, step1))
    (outgoing,) = call(owner_forward_body, [(PIECES, F32)], (owned,), 2**17, MIB // 2)
    arrived = swap(outgoing, ROWS)
    (twice,) = call(add_body, [(HALF, F32)], (pair, step1), 2**16, MIB, after=(outgoing,))
    step2 = lax.ppermute(twice, "x", [(0, 3), (1, 2)])
    (wide,) = call(
        collect_body,
        [((2,) + HALF, F32)],
        (step1, step2),
        2**16,
        MIB,
    )
    mixed, low, q_turned = call(
        near_body,
        [((NH, 2, HD, TOK), F32), (STACKED, BF16), (TURNED, BF16)],
        (
            rates, norm_gain, both_cores(wide), both, queries, key_rows, value_rows, grad_normed,
        ),
        2**28,
        4 * MIB,
        tuple(range(8)),
        tuple(range(3)),
        ALONE,
        views={3: (MATRIX, lambda ref: ref.at[0])},
    )
    attended, high, payload = call(
        attend_body,
        [(TURNED, F32), (STACKED, BF16), ((8, 8, HD), F32)],
        (both_cores(arrived), rates, mixed, q_turned),
        2**27,
        4 * MIB,
    )
    sums = swap(payload, "heads")
    own, send, keep, give = call(
        grad_body,
        [
            (PIECES, F32),
            (PIECES, F32),
            ((PLANE,) + HALF, F32),
            ((PLANE,) + HALF, F32),
        ],
        (sums, rates, attended, mixed, q_turned),
        2**28,
        6 * MIB,
    )
    (joined,) = call(pair_body, [(PIECES, F32)], (own, both_cores(send)), 2**17, 3 * MIB // 2)
    returned = swap(joined, ROWS)
    given = both_cores(give)
    first, second = call(join_body, [(HALF, F32), (HALF, F32)], (keep, given), 2**17, MIB)
    back2 = lax.ppermute(second, "x", [(3, 0), (2, 1)])
    normed, grad_q, near_k, near_v, grad_rates = call(
        back_body,
        [(TOKENS, BF16), (TOKENS, BF16), (TOKENS, F32), (TOKENS, F32), ((LOCAL + FAR, NH, TOK), F32)],
        (
            sums, norm_gain, rates, queries, key_rows, value_rows, mixed, attended, low, high,
        ),
        2**28,
        5 * MIB,
        tuple(range(10)),
        tuple(range(5)),
        ALONE,
        views={6: (TURNED, lambda ref: ref.at[:, 1])},
    )
    returned, back2 = lax.optimization_barrier((returned, back2))
    (spread,) = call(owner_backward_body, [((64, 8, HD), F32)], (returned,), 2**17, MIB // 2)
    total = swap(spread, CTX).reshape(MATRIX)
    (onward,) = call(add_odd_body, [(HALF, F32)], (first, back2), 2**16, MIB, after=(spread,))
    back1 = lax.ppermute(onward, "x", [(0, 1), (1, 0), (3, 2)])
    mine, theirs = call(
        merge_body, [(HALF, F32), (HALF, F32)], (back1, back2, keep, given), 2**16, MIB
    )
    grad_k, grad_v = call(
        final_body,
        [(TOKENS, BF16), (TOKENS, BF16)],
        (total, mine, both_cores(theirs), key_rows, value_rows, near_k, near_v),
        2**26,
        3 * MIB,
    )
    return normed, grad_q, grad_k, grad_v, jnp.transpose(grad_rates, (1, 0, 2))


def solution(mesh):
    grid = Mesh(mesh.devices.reshape(8, 8, 4, 2), ("heads",) + CTX)
    rows = P("heads", CTX, None)
    rates = P("heads", None, CTX)
    return jax.shard_map(
        shards,
        mesh=grid,
        in_specs=(rows, rows, rows, rates, P("heads", None), rows),
        out_specs=(rows, rows, rows, rows, rates),
        check_vma=False,
    )
```

```python
import math

import jax
import jax.numpy as jnp
from jax import lax
from jax.experimental import pallas as pl
from jax.experimental.pallas import tpu as pltpu
from jax.sharding import Mesh
from jax.sharding import PartitionSpec as P

EPS = 1e-06
F32 = jnp.float32
BF16 = jnp.bfloat16

NH = 4
TOK = 256
HD = 128
LOCAL = 9
FAR = 6
PLANE = 3
WIDTH = 32 * HD
MIB = 2**20
ALONE = 60

CTX = ("z", "x", "core")
ROWS = ("z", "x")

TOKENS = (NH, TOK, HD)
TURNED = (NH, HD, TOK)
MATRIX = (NH, HD, HD)
HALF = (NH // 2, HD, HD)
STACKED = (NH, PLANE * HD, HD)
PIECES = (32, PLANE, 8, HD)


def level_scale(number):
    return 2.0 ** (-max(number - 1, 0) / 2.0) / math.sqrt(HD)


def dot(a, b, ca, cb):
    return lax.dot_general(a, b, (((ca,), (cb,)), ((), ())), preferred_element_type=F32)


def call(body, outs, operands, flops, moved, far_in=(), far_out=(), limit=16, after=(), views={}):
    near = pl.BlockSpec(memory_space=pltpu.VMEM)
    far = pl.BlockSpec(memory_space=pltpu.HBM)
    count = len(operands)
    shapes = [views[i][0] if i in views else a.shape for i, a in enumerate(operands)]
    buffers = [pltpu.VMEM(shapes[i], operands[i].dtype) for i in far_in]
    buffers += [pltpu.VMEM(*outs[i]) for i in far_out]

    def split(shape):
        return shape[0] == NH and len(shape) > 2

    parts = [NH if split(shapes[i]) else 1 for i in far_in]
    parts += [NH if split(outs[i][0]) else 1 for i in far_out]
    copies = sum(parts)

    def wrapped(*refs):
        refs = list(refs)
        sems = refs.pop() if copies else None
        del refs[count : count + len(after)]
        scratch = refs[count + len(outs) :]
        used = refs[: count + len(outs)]
        whole, before, behind, last = [], [[] for _ in range(NH)], [[] for _ in range(NH)], []
        sem = 0
        for slot, i in enumerate(far_in):
            held = scratch[slot]
            if i in views:
                used[i] = views[i][1](used[i])
            if parts[slot] == NH:
                for h in range(NH):
                    before[h].append(
                        pltpu.make_async_copy(used[i].at[h], held.at[h], sems.at[sem + h])
                    )
            else:
                whole.append(pltpu.make_async_copy(used[i], held, sems.at[sem]))
            sem += parts[slot]
            used[i] = held
        for slot, i in enumerate(far_out, len(far_in)):
            held = scratch[slot]
            if parts[slot] == NH:
                for h in range(NH):
                    behind[h].append(
                        pltpu.make_async_copy(held.at[h], used[count + i].at[h], sems.at[sem + h])
                    )
            else:
                last.append(pltpu.make_async_copy(held, used[count + i], sems.at[sem]))
            sem += parts[slot]
            used[count + i] = held
        for copy in whole + sum(before, []):
            copy.start()
        for copy in whole:
            copy.wait()
        step = body(*used)
        for h in range(NH):
            for copy in before[h]:
                copy.wait()
            if step is not None:
                step(h)
            for copy in behind[h]:
                copy.start()
        for copy in last:
            copy.start()
        for copy in sum(behind, []) + last:
            copy.wait()

    return pl.pallas_call(
        wrapped,
        out_shape=[jax.ShapeDtypeStruct(s, d) for s, d in outs],
        in_specs=[far if i in far_in else near for i in range(count)]
        + [pl.BlockSpec(memory_space=pl.ANY)] * len(after),
        out_specs=[far if i in far_out else near for i in range(len(outs))],
        scratch_shapes=buffers + ([pltpu.SemaphoreType.DMA((copies,))] if copies else []),
        cost_estimate=pl.CostEstimate(flops=flops, bytes_accessed=moved, transcendentals=0),
        compiler_params=pltpu.CompilerParams(vmem_limit_bytes=int(limit * MIB)),
    )(*operands, *after)


def key_value_body(k_ref, v_ref, kv_ref):
    def step(h):
        kv_ref[h] = dot(k_ref[h], v_ref[h], 0, 0)

    return step


def level_masks():
    s = lax.broadcasted_iota(jnp.int32, (TOK, TOK), 0)
    t = lax.broadcasted_iota(jnp.int32, (TOK, TOK), 1)
    differ = s ^ t
    bucket = jnp.zeros((TOK, TOK), jnp.int32)
    for exponent in range(LOCAL - 1):
        bucket = bucket + (differ >= 2**exponent).astype(jnp.int32)
    return jnp.where(s <= t, bucket, -1)


def level_row(lw_ref, number, h):
    return lw_ref[number, h : h + 1, :] * level_scale(number)


def near_weights(lw_ref, level, h):
    weights = jnp.zeros((TOK, TOK), F32)
    for number in range(LOCAL):
        weights = jnp.where(level == number, level_row(lw_ref, number, h), weights)
    return weights


def scaled_queries(q_t, lw_ref, part, h):
    levels = [LOCAL + part * PLANE + m for m in range(PLANE)]
    return jnp.concatenate([q_t * level_row(lw_ref, n, h) for n in levels], axis=0).astype(BF16)


def near_body(
    lw_ref, gain_ref, wide_ref, both_ref, q_ref, k_ref, v_ref, gn_ref, mixed_ref, st_ref, qt_ref
):
    level = level_masks()
    odd = lax.axis_index("core") == 1

    def step(h):
        q = q_ref[h]
        scores = dot(k_ref[h], q, 1, 1)
        weighted = (near_weights(lw_ref, level, h) * scores).astype(BF16)
        q_t = q.astype(F32).T
        qt_ref[h] = q_t.astype(BF16)
        s0 = jnp.where(odd, both_ref[h], jnp.float32(0.0))
        s1 = wide_ref[h // 2, 0, h % 2]
        s2 = wide_ref[h // 2, 1, h % 2]
        states = jnp.concatenate([s0, s1, s2], axis=0).astype(BF16)
        st_ref[h] = states
        far = dot(states, scaled_queries(q_t, lw_ref, 0, h), 0, 0)
        mixed_ref[h, 0] = dot(v_ref[h], weighted, 0, 0) + far
        mixed_ref[h, 1] = (gain_ref[h : h + 1, :] * gn_ref[h].astype(F32)).T

    return step


def half_body(both_ref, out_ref):
    first = lax.axis_index("core") * (NH // 2)
    for h in range(NH // 2):
        out_ref[h] = both_ref[0, first + h] + both_ref[1, first + h]


def collect_body(step1_ref, step2_ref, out_ref):
    odd = (lax.axis_index("x") & 1) == 1
    for h in range(NH // 2):
        out_ref[0, h] = jnp.where(odd, step1_ref[h], jnp.float32(0.0))
        out_ref[1, h] = step2_ref[h]


def add_body(a_ref, b_ref, out_ref):
    out_ref[...] = a_ref[...] + b_ref[...]


def add_odd_body(a_ref, b_ref, out_ref):
    odd = (lax.axis_index("x") & 1) == 1
    out_ref[...] = jnp.where(odd, a_ref[...], jnp.float32(0.0)) + b_ref[...]


def owner_forward_body(in_ref, out_ref):
    sums = []
    for z in range(8):
        total = in_ref[8 * z]
        for p in range(1, 8):
            total = total + in_ref[8 * z + p]
        sums.append(total)
    nothing = jnp.zeros((8, HD), F32)
    pair0 = sums[0] + sums[1]
    pair2 = sums[4] + sums[5]
    four = pair0 + (sums[2] + sums[3])
    for z in range(8):
        first = sums[z - 1] if z & 1 else nothing
        second = (pair2 if z & 4 else pair0) if z & 2 else nothing
        third = four if z & 4 else nothing
        for x in range(4):
            out_ref[4 * z + x, 0] = first
            out_ref[4 * z + x, 1] = second
            out_ref[4 * z + x, 2] = third


def far_states(pc_ref, h):
    tiles = []
    for m in range(PLANE):
        for i in range(16):
            tiles.append(pc_ref[i % 2, 8 * h + i // 2, m])
    return jnp.concatenate(tiles, axis=0).astype(BF16)


def attend_body(pc_ref, lw_ref, q_ref, mixed_ref, att_ref, pay_ref):
    squares = jnp.zeros((HD, TOK), F32)
    inner = jnp.zeros((HD, TOK), F32)
    for h in range(NH):
        states = far_states(pc_ref, h)
        att = mixed_ref[h, 0]
        for m in range(PLANE):
            far = dot(states[m * HD : (m + 1) * HD], q_ref[h], 0, 1)
            att = att + level_row(lw_ref, LOCAL + PLANE + m, h) * far
        att_ref[h] = att
        squares = squares + att * att
        inner = inner + mixed_ref[h, 1] * att
    squares = jnp.sum(squares, axis=0, keepdims=True)
    inner = jnp.sum(inner, axis=0, keepdims=True)
    rows = [squares[:, :HD], squares[:, HD:], inner[:, :HD], inner[:, HD:]]
    tile = jnp.concatenate(rows + [jnp.zeros((4, HD), F32)], axis=0)
    for peer in range(8):
        pay_ref[peer] = tile


def token_rows(recv_ref):
    total = recv_ref[0]
    for peer in range(1, 8):
        total = total + recv_ref[peer]
    inv = lax.rsqrt(total[0:2] / WIDTH + EPS)
    coef = inv * inv * inv * total[2:4] / WIDTH
    inv_row = jnp.concatenate([inv[0:1], inv[1:2]], axis=1)
    coef_row = jnp.concatenate([coef[0:1], coef[1:2]], axis=1)
    return inv_row, coef_row


def grad_body(
    recv_ref, lw_ref, att_ref, mixed_ref, qt_ref, own_ref, send_ref, keep_ref, give_ref
):
    first = lax.axis_index("core") == 0
    inv_row, coef_row = token_rows(recv_ref)
    for h in range(NH):
        go = (inv_row * mixed_ref[h, 1] - att_ref[h] * coef_row).astype(BF16)
        q_t = qt_ref[h].astype(F32)
        states = dot(scaled_queries(q_t, lw_ref, 1, h), go, 1, 1)
        for m in range(PLANE):
            for k in range(8):
                row = m * HD + 16 * k
                even = states[row : row + 8]
                odd = states[row + 8 : row + 16]
                own_ref[8 * h + k, m] = jnp.where(first, even, odd)
                send_ref[8 * h + k, m] = jnp.where(first, odd, even)
        states = dot(scaled_queries(q_t, lw_ref, 0, h), go, 1, 1)
        mine = first if h < NH // 2 else jnp.logical_not(first)
        for m in range(PLANE):
            value = states[m * HD : (m + 1) * HD]

            @pl.when(mine)
            def _keep(value=value, m=m, h=h):
                keep_ref[m, h % 2] = value

            @pl.when(jnp.logical_not(mine))
            def _give(value=value, m=m, h=h):
                give_ref[m, h % 2] = value


def pair_body(own_ref, gath_ref, out_ref):
    other = 1 - lax.axis_index("core")
    out_ref[...] = own_ref[...] + gath_ref[other]


def join_body(keep_ref, gath_ref, first_ref, second_ref):
    other = 1 - lax.axis_index("core")
    for h in range(NH // 2):
        first_ref[h] = keep_ref[1, h] + gath_ref[other, 1, h]
        second_ref[h] = keep_ref[2, h] + gath_ref[other, 2, h]


def merge_body(back1_ref, back2_ref, keep_ref, gath_ref, mine_ref, send_ref):
    first = lax.axis_index("core") == 0
    zero = jnp.float32(0.0)
    for h in range(NH // 2):
        total = back1_ref[h] + back2_ref[h]
        mine_ref[h] = total + jnp.where(first, gath_ref[1, 0, h], zero)
        send_ref[h] = total + jnp.where(first, zero, keep_ref[0, h])


def owner_backward_body(in_ref, out_ref):
    grads = []
    for m in range(PLANE):
        rows = []
        for z in range(8):
            total = in_ref[4 * z, m]
            for x in range(1, 4):
                total = total + in_ref[4 * z + x, m]
            rows.append(total)
        grads.append(rows)
    pair2 = grads[1][2] + grads[1][3]
    pair6 = grads[1][6] + grads[1][7]
    four = (grads[2][4] + grads[2][5]) + (grads[2][6] + grads[2][7])
    for z in range(8):
        total = jnp.zeros((8, HD), F32)
        if not z & 1:
            total = total + grads[0][z + 1]
        if not z & 2:
            total = total + (pair6 if z & 4 else pair2)
        if not z & 4:
            total = total + four
        for p in range(8):
            out_ref[8 * z + p] = total


def back_body(
    recv_ref, gain_ref, lw_ref, q_ref, k_ref, v_ref, mixed_ref, att_ref, low_ref, pc_ref,
    nm_ref, gq_ref, gk_ref, gv_ref, gl_ref,
):
    level = level_masks()
    inv_row, coef_row = token_rows(recv_ref)

    def step(h):
        q, k, att = q_ref[h], k_ref[h], att_ref[h]
        go = (inv_row * mixed_ref[h] - att * coef_row).astype(BF16)
        nm_ref[h] = ((att * inv_row).T * gain_ref[h : h + 1, :]).astype(BF16)
        scores = dot(k, q, 1, 1)
        weights = near_weights(lw_ref, level, h)
        mix = dot(v_ref[h], go, 1, 0)
        gv_ref[h] = dot((weights * scores).astype(BF16), go, 1, 1)
        grad_scores = (weights * mix).astype(BF16)
        gk_ref[h] = dot(grad_scores, q, 1, 0)
        product = mix * scores
        rows = []
        for number in range(LOCAL):
            picked = jnp.where(level == number, product, jnp.float32(0.0))
            rows.append(level_scale(number) * jnp.sum(picked, axis=0, keepdims=True))
        q_t = q.astype(F32).T
        far_t = dot(k, grad_scores, 0, 0)
        for part in range(2):
            turned = dot(far_states(pc_ref, h) if part else low_ref[h], go, 1, 0)
            for m in range(PLANE):
                piece = turned[m * HD : (m + 1) * HD]
                number = LOCAL + part * PLANE + m
                far_t = far_t + level_row(lw_ref, number, h) * piece
                rows.append(level_scale(number) * jnp.sum(piece * q_t, axis=0, keepdims=True))
        gq_ref[h] = far_t.T.astype(BF16)
        for number in range(LOCAL + FAR):
            gl_ref[number, h : h + 1, :] = rows[number]

    return step


def final_body(piece_ref, mine_ref, wide_ref, k_ref, v_ref, gk_ref, gv_ref, outk_ref, outv_ref):
    first = lax.axis_index("core") == 0

    def step(h):
        mine = first if h < NH // 2 else jnp.logical_not(first)
        plane = jnp.where(mine, mine_ref[h % 2], wide_ref[h // 2, h % 2])
        grad_kv = (piece_ref[h] + plane).astype(BF16)
        outk_ref[h] = (gk_ref[h] + dot(v_ref[h], grad_kv, 1, 1)).astype(BF16)
        outv_ref[h] = (gv_ref[h] + dot(k_ref[h], grad_kv, 1, 0)).astype(BF16)

    return step


def swap(value, axes):
    return lax.all_to_all(value, axes, split_axis=0, concat_axis=0, tiled=True)


def both_cores(value):
    return lax.all_gather(value, "core", axis=0, tiled=False)


def shards(queries, key_rows, value_rows, level_weights, norm_gain, grad_normed):
    rates = jnp.transpose(level_weights, (1, 0, 2))
    (kv,) = call(
        key_value_body, [(MATRIX, F32)], (key_rows, value_rows), 2**25, MIB, (0, 1), (), ALONE
    )
    owned = swap(kv.reshape(64, 8, HD), CTX)
    both = both_cores(kv)
    (pair,) = call(half_body, [(HALF, F32)], (both,), 2**16, MIB)
    step1 = lax.ppermute(pair, "x", [(0, 1), (1, 0), (2, 3), (3, 2)])
    owned, step1 = lax.optimization_barrier((owned, step1))
    (outgoing,) = call(owner_forward_body, [(PIECES, F32)], (owned,), 2**17, MIB // 2)
    arrived = swap(outgoing, ROWS)
    (twice,) = call(add_body, [(HALF, F32)], (pair, step1), 2**16, MIB, after=(outgoing,))
    step2 = lax.ppermute(twice, "x", [(0, 3), (1, 2)])
    (wide,) = call(
        collect_body,
        [((2,) + HALF, F32)],
        (step1, step2),
        2**16,
        MIB,
    )
    mixed, low, q_turned = call(
        near_body,
        [((NH, 2, HD, TOK), F32), (STACKED, BF16), (TURNED, BF16)],
        (
            rates, norm_gain, both_cores(wide), both, queries, key_rows, value_rows, grad_normed,
        ),
        2**34,
        4 * MIB,
        tuple(range(8)),
        tuple(range(3)),
        ALONE,
        views={3: (MATRIX, lambda ref: ref.at[0])},
    )
    gathered = both_cores(arrived)
    attended, payload = call(
        attend_body,
        [(TURNED, F32), ((8, 8, HD), F32)],
        (gathered, rates, queries, mixed),
        2**27,
        4 * MIB,
    )
    sums = swap(payload, "heads")
    own, send, keep, give = call(
        grad_body,
        [
            (PIECES, F32),
            (PIECES, F32),
            ((PLANE,) + HALF, F32),
            ((PLANE,) + HALF, F32),
        ],
        (sums, rates, attended, mixed, q_turned),
        2**28,
        6 * MIB,
    )
    (joined,) = call(pair_body, [(PIECES, F32)], (own, both_cores(send)), 2**17, 3 * MIB // 2)
    returned = swap(joined, ROWS)
    given = both_cores(give)
    first, second = call(join_body, [(HALF, F32), (HALF, F32)], (keep, given), 2**17, MIB)
    back2 = lax.ppermute(second, "x", [(3, 0), (2, 1)])
    normed, grad_q, near_k, near_v, grad_rates = call(
        back_body,
        [(TOKENS, BF16), (TOKENS, BF16), (TOKENS, F32), (TOKENS, F32), ((LOCAL + FAR, NH, TOK), F32)],
        (
            sums, norm_gain, rates, queries, key_rows, value_rows, mixed, attended, low, gathered,
        ),
        2**34,
        5 * MIB,
        tuple(range(10)),
        tuple(range(5)),
        ALONE,
        views={6: (TURNED, lambda ref: ref.at[:, 1])},
    )
    returned, back2, near_k = lax.optimization_barrier((returned, back2, near_k))
    (spread,) = call(owner_backward_body, [((64, 8, HD), F32)], (returned,), 2**17, MIB // 2)
    total = swap(spread, CTX).reshape(MATRIX)
    (onward,) = call(add_odd_body, [(HALF, F32)], (first, back2), 2**16, MIB, after=(spread,))
    back1 = lax.ppermute(onward, "x", [(0, 1), (1, 0), (3, 2)])
    mine, theirs = call(
        merge_body, [(HALF, F32), (HALF, F32)], (back1, back2, keep, given), 2**16, MIB
    )
    grad_k, grad_v = call(
        final_body,
        [(TOKENS, BF16), (TOKENS, BF16)],
        (total, mine, both_cores(theirs), key_rows, value_rows, near_k, near_v),
        2**26,
        3 * MIB,
    )
    return normed, grad_q, grad_k, grad_v, jnp.transpose(grad_rates, (1, 0, 2))


def solution(mesh):
    grid = Mesh(mesh.devices.reshape(8, 8, 4, 2), ("heads",) + CTX)
    rows = P("heads", CTX, None)
    rates = P("heads", None, CTX)
    return jax.shard_map(
        shards,
        mesh=grid,
        in_specs=(rows, rows, rows, rates, P("heads", None), rows),
        out_specs=(rows, rows, rows, rows, rates),
        check_vma=False,
    )
```

```python
import math

import jax
import jax.numpy as jnp
from jax import lax
from jax.experimental import pallas as pl
from jax.experimental.pallas import tpu as pltpu
from jax.sharding import Mesh
from jax.sharding import PartitionSpec as P

EPS = 1e-06
F32 = jnp.float32
BF16 = jnp.bfloat16

NH = 4
TOK = 256
HD = 128
LOCAL = 9
FAR = 6
PLANE = 3
WIDTH = 32 * HD
MIB = 2**20
ALONE = 60

CTX = ("z", "x", "core")
ROWS = ("z", "x")

TOKENS = (NH, TOK, HD)
TURNED = (NH, HD, TOK)
MATRIX = (NH, HD, HD)
HALF = (NH // 2, HD, HD)
STACKED = (NH, PLANE * HD, HD)
PIECES = (32, PLANE, 8, HD)


def level_scale(number):
    return 2.0 ** (-max(number - 1, 0) / 2.0) / math.sqrt(HD)


def dot(a, b, ca, cb):
    return lax.dot_general(a, b, (((ca,), (cb,)), ((), ())), preferred_element_type=F32)


def call(body, outs, operands, flops, moved, far_in=(), far_out=(), limit=16, after=(), views={}, whole_in=False):
    near = pl.BlockSpec(memory_space=pltpu.VMEM)
    far = pl.BlockSpec(memory_space=pltpu.HBM)
    count = len(operands)
    shapes = [views[i][0] if i in views else a.shape for i, a in enumerate(operands)]
    buffers = [pltpu.VMEM(shapes[i], operands[i].dtype) for i in far_in]
    buffers += [pltpu.VMEM(*outs[i]) for i in far_out]

    def split(shape):
        return shape[0] == NH and len(shape) > 2

    parts = [NH if split(shapes[i]) and not whole_in else 1 for i in far_in]
    parts += [NH if split(outs[i][0]) else 1 for i in far_out]
    copies = sum(parts)

    def wrapped(*refs):
        refs = list(refs)
        sems = refs.pop() if copies else None
        del refs[count : count + len(after)]
        scratch = refs[count + len(outs) :]
        used = refs[: count + len(outs)]
        whole, before, behind, last = [], [[] for _ in range(NH)], [[] for _ in range(NH)], []
        sem = 0
        for slot, i in enumerate(far_in):
            held = scratch[slot]
            if i in views:
                used[i] = views[i][1](used[i])
            if parts[slot] == NH:
                for h in range(NH):
                    before[h].append(
                        pltpu.make_async_copy(used[i].at[h], held.at[h], sems.at[sem + h])
                    )
            else:
                whole.append(pltpu.make_async_copy(used[i], held, sems.at[sem]))
            sem += parts[slot]
            used[i] = held
        for slot, i in enumerate(far_out, len(far_in)):
            held = scratch[slot]
            if parts[slot] == NH:
                for h in range(NH):
                    behind[h].append(
                        pltpu.make_async_copy(held.at[h], used[count + i].at[h], sems.at[sem + h])
                    )
            else:
                last.append(pltpu.make_async_copy(held, used[count + i], sems.at[sem]))
            sem += parts[slot]
            used[count + i] = held
        for copy in whole + sum(before, []):
            copy.start()
        for copy in whole:
            copy.wait()
        step = body(*used)
        for h in range(NH):
            for copy in before[h]:
                copy.wait()
            if step is not None:
                step(h)
            for copy in behind[h]:
                copy.start()
        for copy in last:
            copy.start()
        for copy in sum(behind, []) + last:
            copy.wait()

    return pl.pallas_call(
        wrapped,
        out_shape=[jax.ShapeDtypeStruct(s, d) for s, d in outs],
        in_specs=[far if i in far_in else near for i in range(count)]
        + [pl.BlockSpec(memory_space=pl.ANY)] * len(after),
        out_specs=[far if i in far_out else near for i in range(len(outs))],
        scratch_shapes=buffers + ([pltpu.SemaphoreType.DMA((copies,))] if copies else []),
        cost_estimate=pl.CostEstimate(flops=flops, bytes_accessed=moved, transcendentals=0),
        compiler_params=pltpu.CompilerParams(vmem_limit_bytes=int(limit * MIB)),
    )(*operands, *after)


def key_value_body(k_ref, v_ref, kv_ref):
    def step(h):
        kv_ref[h] = dot(k_ref[h], v_ref[h], 0, 0)

    return step


def level_masks():
    s = lax.broadcasted_iota(jnp.int32, (TOK, TOK), 0)
    t = lax.broadcasted_iota(jnp.int32, (TOK, TOK), 1)
    differ = s ^ t
    bucket = jnp.zeros((TOK, TOK), jnp.int32)
    for exponent in range(LOCAL - 1):
        bucket = bucket + (differ >= 2**exponent).astype(jnp.int32)
    return jnp.where(s <= t, bucket, -1)


def level_row(lw_ref, number, h):
    return lw_ref[number, h : h + 1, :] * level_scale(number)


def near_weights(lw_ref, level, h):
    weights = jnp.zeros((TOK, TOK), F32)
    for number in range(LOCAL):
        weights = jnp.where(level == number, level_row(lw_ref, number, h), weights)
    return weights


def scaled_queries(q_t, lw_ref, part, h):
    levels = [LOCAL + part * PLANE + m for m in range(PLANE)]
    return jnp.concatenate([q_t * level_row(lw_ref, n, h) for n in levels], axis=0).astype(BF16)


def near_body(
    lw_ref, gain_ref, wide_ref, both_ref, q_ref, k_ref, v_ref, gn_ref, mixed_ref, st_ref, qt_ref
):
    level = level_masks()
    odd = lax.axis_index("core") == 1

    def step(h):
        q = q_ref[h]
        scores = dot(k_ref[h], q, 1, 1)
        weighted = (near_weights(lw_ref, level, h) * scores).astype(BF16)
        q_t = q.astype(F32).T
        qt_ref[h] = q_t.astype(BF16)
        s0 = jnp.where(odd, both_ref[h], jnp.float32(0.0))
        s1 = wide_ref[h // 2, 0, h % 2]
        s2 = wide_ref[h // 2, 1, h % 2]
        states = jnp.concatenate([s0, s1, s2], axis=0).astype(BF16)
        st_ref[h] = states
        far = dot(states, scaled_queries(q_t, lw_ref, 0, h), 0, 0)
        mixed_ref[h, 0] = dot(v_ref[h], weighted, 0, 0) + far
        mixed_ref[h, 1] = (gain_ref[h : h + 1, :] * gn_ref[h].astype(F32)).T

    return step


def half_body(both_ref, out_ref):
    first = lax.axis_index("core") * (NH // 2)
    for h in range(NH // 2):
        out_ref[h] = both_ref[0, first + h] + both_ref[1, first + h]


def collect_body(step1_ref, step2_ref, out_ref):
    odd = (lax.axis_index("x") & 1) == 1
    for h in range(NH // 2):
        out_ref[0, h] = jnp.where(odd, step1_ref[h], jnp.float32(0.0))
        out_ref[1, h] = step2_ref[h]


def add_body(a_ref, b_ref, out_ref):
    out_ref[...] = a_ref[...] + b_ref[...]


def add_odd_body(a_ref, b_ref, out_ref):
    odd = (lax.axis_index("x") & 1) == 1
    out_ref[...] = jnp.where(odd, a_ref[...], jnp.float32(0.0)) + b_ref[...]


def owner_forward_body(in_ref, out_ref):
    sums = []
    for z in range(8):
        total = in_ref[8 * z]
        for p in range(1, 8):
            total = total + in_ref[8 * z + p]
        sums.append(total)
    nothing = jnp.zeros((8, HD), F32)
    pair0 = sums[0] + sums[1]
    pair2 = sums[4] + sums[5]
    four = pair0 + (sums[2] + sums[3])
    for z in range(8):
        first = sums[z - 1] if z & 1 else nothing
        second = (pair2 if z & 4 else pair0) if z & 2 else nothing
        third = four if z & 4 else nothing
        for x in range(4):
            out_ref[4 * z + x, 0] = first
            out_ref[4 * z + x, 1] = second
            out_ref[4 * z + x, 2] = third


def far_states(pc_ref, h):
    tiles = []
    for m in range(PLANE):
        for i in range(16):
            tiles.append(pc_ref[i % 2, 8 * h + i // 2, m])
    return jnp.concatenate(tiles, axis=0).astype(BF16)


def attend_body(pc_ref, lw_ref, q_ref, mixed_ref, att_ref, pay_ref):
    squares = jnp.zeros((HD, TOK), F32)
    inner = jnp.zeros((HD, TOK), F32)
    for h in range(NH):
        states = far_states(pc_ref, h)
        att = mixed_ref[h, 0]
        for m in range(PLANE):
            far = dot(states[m * HD : (m + 1) * HD], q_ref[h], 0, 1)
            att = att + level_row(lw_ref, LOCAL + PLANE + m, h) * far
        att_ref[h] = att
        squares = squares + att * att
        inner = inner + mixed_ref[h, 1] * att
    squares = jnp.sum(squares, axis=0, keepdims=True)
    inner = jnp.sum(inner, axis=0, keepdims=True)
    rows = [squares[:, :HD], squares[:, HD:], inner[:, :HD], inner[:, HD:]]
    tile = jnp.concatenate(rows, axis=0)
    for peer in range(8):
        pay_ref[peer] = tile


def token_rows(recv_ref):
    total = recv_ref[0]
    for peer in range(1, 8):
        total = total + recv_ref[peer]
    inv = lax.rsqrt(total[0:2] / WIDTH + EPS)
    coef = inv * inv * inv * total[2:4] / WIDTH
    inv_row = jnp.concatenate([inv[0:1], inv[1:2]], axis=1)
    coef_row = jnp.concatenate([coef[0:1], coef[1:2]], axis=1)
    return inv_row, coef_row


def grad_body(
    recv_ref, lw_ref, att_ref, mixed_ref, qt_ref, own_ref, send_ref, keep_ref, give_ref
):
    first = lax.axis_index("core") == 0
    inv_row, coef_row = token_rows(recv_ref)
    for h in range(NH):
        go = (inv_row * mixed_ref[h, 1] - att_ref[h] * coef_row).astype(BF16)
        q_t = qt_ref[h].astype(F32)
        states = dot(scaled_queries(q_t, lw_ref, 1, h), go, 1, 1)
        for m in range(PLANE):
            for k in range(8):
                row = m * HD + 16 * k
                even = states[row : row + 8]
                odd = states[row + 8 : row + 16]
                own_ref[8 * h + k, m] = jnp.where(first, even, odd)
                send_ref[8 * h + k, m] = jnp.where(first, odd, even)
        states = dot(scaled_queries(q_t, lw_ref, 0, h), go, 1, 1)
        mine = first if h < NH // 2 else jnp.logical_not(first)
        for m in range(PLANE):
            value = states[m * HD : (m + 1) * HD]

            @pl.when(mine)
            def _keep(value=value, m=m, h=h):
                keep_ref[m, h % 2] = value

            @pl.when(jnp.logical_not(mine))
            def _give(value=value, m=m, h=h):
                give_ref[m, h % 2] = value


def pair_body(own_ref, gath_ref, out_ref):
    other = 1 - lax.axis_index("core")
    out_ref[...] = own_ref[...] + gath_ref[other]


def join_body(keep_ref, gath_ref, first_ref, second_ref):
    other = 1 - lax.axis_index("core")
    for h in range(NH // 2):
        first_ref[h] = keep_ref[1, h] + gath_ref[other, 1, h]
        second_ref[h] = keep_ref[2, h] + gath_ref[other, 2, h]


def merge_body(back1_ref, back2_ref, keep_ref, gath_ref, mine_ref, send_ref):
    first = lax.axis_index("core") == 0
    zero = jnp.float32(0.0)
    for h in range(NH // 2):
        total = back1_ref[h] + back2_ref[h]
        mine_ref[h] = total + jnp.where(first, gath_ref[1, 0, h], zero)
        send_ref[h] = total + jnp.where(first, zero, keep_ref[0, h])


def owner_backward_body(in_ref, out_ref):
    grads = []
    for m in range(PLANE):
        rows = []
        for z in range(8):
            total = in_ref[4 * z, m]
            for x in range(1, 4):
                total = total + in_ref[4 * z + x, m]
            rows.append(total)
        grads.append(rows)
    pair2 = grads[1][2] + grads[1][3]
    pair6 = grads[1][6] + grads[1][7]
    four = (grads[2][4] + grads[2][5]) + (grads[2][6] + grads[2][7])
    for z in range(8):
        total = jnp.zeros((8, HD), F32)
        if not z & 1:
            total = total + grads[0][z + 1]
        if not z & 2:
            total = total + (pair6 if z & 4 else pair2)
        if not z & 4:
            total = total + four
        for p in range(8):
            out_ref[8 * z + p] = total


def back_body(
    recv_ref, gain_ref, lw_ref, q_ref, k_ref, v_ref, mixed_ref, att_ref, low_ref, pc_ref,
    nm_ref, gq_ref, gk_ref, gv_ref, gl_ref,
):
    level = level_masks()
    inv_row, coef_row = token_rows(recv_ref)

    def step(h):
        q, k, att = q_ref[h], k_ref[h], att_ref[h]
        go = (inv_row * mixed_ref[h] - att * coef_row).astype(BF16)
        nm_ref[h] = ((att * inv_row).T * gain_ref[h : h + 1, :]).astype(BF16)
        scores = dot(k, q, 1, 1)
        weights = near_weights(lw_ref, level, h)
        mix = dot(v_ref[h], go, 1, 0)
        gv_ref[h] = dot((weights * scores).astype(BF16), go, 1, 1)
        grad_scores = (weights * mix).astype(BF16)
        gk_ref[h] = dot(grad_scores, q, 1, 0)
        product = mix * scores
        rows = []
        for number in range(LOCAL):
            picked = jnp.where(level == number, product, jnp.float32(0.0))
            rows.append(level_scale(number) * jnp.sum(picked, axis=0, keepdims=True))
        q_t = q.astype(F32).T
        far_t = dot(k, grad_scores, 0, 0)
        for part in range(2):
            turned = dot(far_states(pc_ref, h) if part else low_ref[h], go, 1, 0)
            for m in range(PLANE):
                piece = turned[m * HD : (m + 1) * HD]
                number = LOCAL + part * PLANE + m
                far_t = far_t + level_row(lw_ref, number, h) * piece
                rows.append(level_scale(number) * jnp.sum(piece * q_t, axis=0, keepdims=True))
        gq_ref[h] = far_t.T.astype(BF16)
        for number in range(LOCAL + FAR):
            gl_ref[number, h : h + 1, :] = rows[number]

    return step


def final_body(piece_ref, mine_ref, wide_ref, k_ref, v_ref, gk_ref, gv_ref, outk_ref, outv_ref):
    first = lax.axis_index("core") == 0

    def step(h):
        mine = first if h < NH // 2 else jnp.logical_not(first)
        plane = jnp.where(mine, mine_ref[h % 2], wide_ref[h // 2, h % 2])
        grad_kv = (piece_ref[h] + plane).astype(BF16)
        outk_ref[h] = (gk_ref[h] + dot(v_ref[h], grad_kv, 1, 1)).astype(BF16)
        outv_ref[h] = (gv_ref[h] + dot(k_ref[h], grad_kv, 1, 0)).astype(BF16)

    return step


def swap(value, axes):
    return lax.all_to_all(value, axes, split_axis=0, concat_axis=0, tiled=True)


def both_cores(value):
    return lax.all_gather(value, "core", axis=0, tiled=False)


def shards(queries, key_rows, value_rows, level_weights, norm_gain, grad_normed):
    rates = jnp.transpose(level_weights, (1, 0, 2))
    (kv,) = call(
        key_value_body,
        [(MATRIX, F32)],
        (key_rows, value_rows),
        2**25,
        MIB,
        (0, 1),
        (0,),
        ALONE,
        whole_in=True,
    )
    owned = swap(kv.reshape(64, 8, HD), CTX)
    both = both_cores(kv)
    (pair,) = call(half_body, [(HALF, F32)], (both,), 2**16, MIB)
    step1 = lax.ppermute(pair, "x", [(0, 1), (1, 0), (2, 3), (3, 2)])
    (outgoing,) = call(
        owner_forward_body, [(PIECES, F32)], (owned,), 2**17, MIB // 2, after=(pair,)
    )
    arrived = swap(outgoing, ROWS)
    (twice,) = call(add_body, [(HALF, F32)], (pair, step1), 2**16, MIB, after=(outgoing,))
    step2 = lax.ppermute(twice, "x", [(0, 3), (1, 2)])
    (wide,) = call(
        collect_body,
        [((2,) + HALF, F32)],
        (step1, step2),
        2**16,
        MIB,
    )
    mixed, low, q_turned = call(
        near_body,
        [((NH, 2, HD, TOK), F32), (STACKED, BF16), (TURNED, BF16)],
        (
            rates, norm_gain, both_cores(wide), both, queries, key_rows, value_rows, grad_normed,
        ),
        2**34,
        4 * MIB,
        tuple(range(8)),
        tuple(range(3)),
        ALONE,
        views={3: (MATRIX, lambda ref: ref.at[0])},
    )
    gathered = both_cores(arrived)
    attended, payload = call(
        attend_body,
        [(TURNED, F32), ((8, 4, HD), F32)],
        (gathered, rates, queries, mixed),
        2**27,
        4 * MIB,
    )
    sums = swap(payload, "heads")
    own, send, keep, give = call(
        grad_body,
        [
            (PIECES, F32),
            (PIECES, F32),
            ((PLANE,) + HALF, F32),
            ((PLANE,) + HALF, F32),
        ],
        (sums, rates, attended, mixed, q_turned),
        2**28,
        6 * MIB,
    )
    (joined,) = call(pair_body, [(PIECES, F32)], (own, both_cores(send)), 2**17, 3 * MIB // 2)
    returned = swap(joined, ROWS)
    given = both_cores(give)
    first, second = call(join_body, [(HALF, F32), (HALF, F32)], (keep, given), 2**17, MIB)
    back2 = lax.ppermute(second, "x", [(3, 0), (2, 1)])
    normed, grad_q, near_k, near_v, grad_rates = call(
        back_body,
        [(TOKENS, BF16), (TOKENS, BF16), (TOKENS, F32), (TOKENS, F32), ((LOCAL + FAR, NH, TOK), F32)],
        (
            sums, norm_gain, rates, queries, key_rows, value_rows, mixed, attended, low, gathered,
        ),
        2**34,
        5 * MIB,
        tuple(range(10)),
        tuple(range(5)),
        ALONE,
        views={6: (TURNED, lambda ref: ref.at[:, 1])},
    )
    returned, back2, near_k = lax.optimization_barrier((returned, back2, near_k))
    (spread,) = call(owner_backward_body, [((64, 8, HD), F32)], (returned,), 2**17, MIB // 2)
    total = swap(spread, CTX).reshape(MATRIX)
    (onward,) = call(add_odd_body, [(HALF, F32)], (first, back2), 2**16, MIB, after=(spread,))
    back1 = lax.ppermute(onward, "x", [(0, 1), (1, 0), (3, 2)])
    mine, theirs = call(
        merge_body, [(HALF, F32), (HALF, F32)], (back1, back2, keep, given), 2**16, MIB
    )
    grad_k, grad_v = call(
        final_body,
        [(TOKENS, BF16), (TOKENS, BF16)],
        (total, mine, both_cores(theirs), key_rows, value_rows, near_k, near_v),
        2**26,
        3 * MIB,
    )
    return normed, grad_q, grad_k, grad_v, jnp.transpose(grad_rates, (1, 0, 2))


def solution(mesh):
    grid = Mesh(mesh.devices.reshape(8, 8, 4, 2), ("heads",) + CTX)
    rows = P("heads", CTX, None)
    rates = P("heads", None, CTX)
    return jax.shard_map(
        shards,
        mesh=grid,
        in_specs=(rows, rows, rows, rates, P("heads", None), rows),
        out_specs=(rows, rows, rows, rows, rates),
        check_vma=False,
    )
```

```python
import functools
import math

import jax
import jax.numpy as jnp
from jax import lax
from jax.experimental import pallas as pl
from jax.experimental.pallas import tpu as pltpu
from jax.sharding import Mesh
from jax.sharding import PartitionSpec as P

EPS = 1e-06
F32 = jnp.float32
BF16 = jnp.bfloat16

NH = 4
TOK = 256
HD = 128
LOCAL = 9
FAR = 6
PLANE = 3
WIDTH = 32 * HD
MIB = 2**20
ALONE = 60

CTX = ("z", "x", "core")
ROWS = ("z", "x")

TOKENS = (NH, TOK, HD)
TURNED = (NH, HD, TOK)
MATRIX = (NH, HD, HD)
HALF = (NH // 2, HD, HD)
STACKED = (NH, PLANE * HD, HD)
PIECES = (32, PLANE, 8, HD)


def level_scale(number):
    return 2.0 ** (-max(number - 1, 0) / 2.0) / math.sqrt(HD)


def dot(a, b, ca, cb):
    return lax.dot_general(a, b, (((ca,), (cb,)), ((), ())), preferred_element_type=F32)


def call(body, outs, operands, flops, moved, far_in=(), far_out=(), limit=16, after=(), views={}, whole_in=False):
    near = pl.BlockSpec(memory_space=pltpu.VMEM)
    far = pl.BlockSpec(memory_space=pltpu.HBM)
    count = len(operands)
    shapes = [views[i][0] if i in views else a.shape for i, a in enumerate(operands)]
    buffers = [pltpu.VMEM(shapes[i], operands[i].dtype) for i in far_in]
    buffers += [pltpu.VMEM(*outs[i]) for i in far_out]

    def split(shape):
        return shape[0] == NH and len(shape) > 2

    parts = [NH if split(shapes[i]) and not whole_in else 1 for i in far_in]
    parts += [NH if split(outs[i][0]) else 1 for i in far_out]
    copies = sum(parts)

    def wrapped(*refs):
        refs = list(refs)
        sems = refs.pop() if copies else None
        del refs[count : count + len(after)]
        scratch = refs[count + len(outs) :]
        used = refs[: count + len(outs)]
        whole, before, behind, last = [], [[] for _ in range(NH)], [[] for _ in range(NH)], []
        sem = 0
        for slot, i in enumerate(far_in):
            held = scratch[slot]
            if i in views:
                used[i] = views[i][1](used[i])
            if parts[slot] == NH:
                for h in range(NH):
                    before[h].append(
                        pltpu.make_async_copy(used[i].at[h], held.at[h], sems.at[sem + h])
                    )
            else:
                whole.append(pltpu.make_async_copy(used[i], held, sems.at[sem]))
            sem += parts[slot]
            used[i] = held
        for slot, i in enumerate(far_out, len(far_in)):
            held = scratch[slot]
            if parts[slot] == NH:
                for h in range(NH):
                    behind[h].append(
                        pltpu.make_async_copy(held.at[h], used[count + i].at[h], sems.at[sem + h])
                    )
            else:
                last.append(pltpu.make_async_copy(held, used[count + i], sems.at[sem]))
            sem += parts[slot]
            used[count + i] = held
        for copy in whole + sum(before, []):
            copy.start()
        for copy in whole:
            copy.wait()
        step = body(*used)
        for h in range(NH):
            for copy in before[h]:
                copy.wait()
            if step is not None:
                step(h)
            for copy in behind[h]:
                copy.start()
        for copy in last:
            copy.start()
        for copy in sum(behind, []) + last:
            copy.wait()

    return pl.pallas_call(
        wrapped,
        out_shape=[jax.ShapeDtypeStruct(s, d) for s, d in outs],
        in_specs=[far if i in far_in else near for i in range(count)]
        + [pl.BlockSpec(memory_space=pl.ANY)] * len(after),
        out_specs=[far if i in far_out else near for i in range(len(outs))],
        scratch_shapes=buffers + ([pltpu.SemaphoreType.DMA((copies,))] if copies else []),
        cost_estimate=pl.CostEstimate(flops=flops, bytes_accessed=moved, transcendentals=0),
        compiler_params=pltpu.CompilerParams(vmem_limit_bytes=int(limit * MIB)),
    )(*operands, *after)


def key_value_body(k_ref, v_ref, kv_ref):
    def step(h):
        kv_ref[h] = dot(k_ref[h], v_ref[h], 0, 0)

    return step


def level_masks():
    s = lax.broadcasted_iota(jnp.int32, (TOK, TOK), 0)
    t = lax.broadcasted_iota(jnp.int32, (TOK, TOK), 1)
    differ = s ^ t
    bucket = jnp.zeros((TOK, TOK), jnp.int32)
    for exponent in range(LOCAL - 1):
        bucket = bucket + (differ >= 2**exponent).astype(jnp.int32)
    return jnp.where(s <= t, bucket, -1)


def level_row(lw_ref, number, h):
    return lw_ref[number, h : h + 1, :] * level_scale(number)


def near_weights(lw_ref, level, h):
    weights = jnp.zeros((TOK, TOK), F32)
    for number in range(LOCAL):
        weights = jnp.where(level == number, level_row(lw_ref, number, h), weights)
    return weights


def scaled_queries(q_t, lw_ref, part, h):
    levels = [LOCAL + part * PLANE + m for m in range(PLANE)]
    return jnp.concatenate([q_t * level_row(lw_ref, n, h) for n in levels], axis=0).astype(BF16)


def near_body(
    lw_ref, gain_ref, wide_ref, both_ref, q_ref, k_ref, v_ref, gn_ref, mixed_ref, st_ref, qt_ref
):
    level = level_masks()
    odd = lax.axis_index("core") == 1

    def step(h):
        q = q_ref[h]
        scores = dot(k_ref[h], q, 1, 1)
        weighted = (near_weights(lw_ref, level, h) * scores).astype(BF16)
        q_t = q.astype(F32).T
        qt_ref[h] = q_t.astype(BF16)
        s0 = jnp.where(odd, both_ref[h], jnp.float32(0.0))
        s1 = wide_ref[h // 2, 0, h % 2]
        s2 = wide_ref[h // 2, 1, h % 2]
        states = jnp.concatenate([s0, s1, s2], axis=0).astype(BF16)
        st_ref[h] = states
        far = dot(states, scaled_queries(q_t, lw_ref, 0, h), 0, 0)
        mixed_ref[h, 0] = dot(v_ref[h], weighted, 0, 0) + far
        mixed_ref[h, 1] = (gain_ref[h : h + 1, :] * gn_ref[h].astype(F32)).T

    return step


def half_body(both_ref, out_ref):
    first = lax.axis_index("core") * (NH // 2)
    for h in range(NH // 2):
        out_ref[h] = both_ref[0, first + h] + both_ref[1, first + h]


def collect_body(step1_ref, step2_ref, out_ref):
    odd = (lax.axis_index("x") & 1) == 1
    for h in range(NH // 2):
        out_ref[0, h] = jnp.where(odd, step1_ref[h], jnp.float32(0.0))
        out_ref[1, h] = step2_ref[h]


def add_body(a_ref, b_ref, out_ref):
    out_ref[...] = a_ref[...] + b_ref[...]


def add_odd_body(a_ref, b_ref, out_ref):
    odd = (lax.axis_index("x") & 1) == 1
    out_ref[...] = jnp.where(odd, a_ref[...], jnp.float32(0.0)) + b_ref[...]


def owner_forward_body(in_ref, out_ref):
    sums = []
    for z in range(8):
        total = in_ref[4 * z]
        for x in range(1, 4):
            total = total + in_ref[4 * z + x]
        sums.append(total)
    nothing = jnp.zeros((8, HD), F32)
    pair0 = sums[0] + sums[1]
    pair2 = sums[4] + sums[5]
    four = pair0 + (sums[2] + sums[3])
    for z in range(8):
        first = sums[z - 1] if z & 1 else nothing
        second = (pair2 if z & 4 else pair0) if z & 2 else nothing
        third = four if z & 4 else nothing
        for x in range(4):
            out_ref[4 * z + x, 0] = first
            out_ref[4 * z + x, 1] = second
            out_ref[4 * z + x, 2] = third


def far_states(pc_ref, h):
    tiles = []
    for m in range(PLANE):
        for i in range(16):
            tiles.append(pc_ref[h // 2, 16 * (h % 2) + i, m])
    return jnp.concatenate(tiles, axis=0).astype(BF16)


def attend_body(pc_ref, lw_ref, q_ref, mixed_ref, att_ref, pay_ref):
    squares = jnp.zeros((HD, TOK), F32)
    inner = jnp.zeros((HD, TOK), F32)
    for h in range(NH):
        states = far_states(pc_ref, h)
        att = mixed_ref[h, 0]
        for m in range(PLANE):
            far = dot(states[m * HD : (m + 1) * HD], q_ref[h], 0, 1)
            att = att + level_row(lw_ref, LOCAL + PLANE + m, h) * far
        att_ref[h] = att
        squares = squares + att * att
        inner = inner + mixed_ref[h, 1] * att
    squares = jnp.sum(squares, axis=0, keepdims=True)
    inner = jnp.sum(inner, axis=0, keepdims=True)
    rows = [squares[:, :HD], squares[:, HD:], inner[:, :HD], inner[:, HD:]]
    tile = jnp.concatenate(rows, axis=0)
    for peer in range(8):
        pay_ref[peer] = tile


def token_rows(recv_ref):
    total = recv_ref[0]
    for peer in range(1, 8):
        total = total + recv_ref[peer]
    inv = lax.rsqrt(total[0:2] / WIDTH + EPS)
    coef = inv * inv * inv * total[2:4] / WIDTH
    inv_row = jnp.concatenate([inv[0:1], inv[1:2]], axis=1)
    coef_row = jnp.concatenate([coef[0:1], coef[1:2]], axis=1)
    return inv_row, coef_row


def grad_body(
    recv_ref, lw_ref, att_ref, mixed_ref, qt_ref, own_ref, send_ref, keep_ref, give_ref
):
    first = lax.axis_index("core") == 0
    inv_row, coef_row = token_rows(recv_ref)
    for h in range(NH):
        go = (inv_row * mixed_ref[h, 1] - att_ref[h] * coef_row).astype(BF16)
        q_t = qt_ref[h].astype(F32)
        far = dot(scaled_queries(q_t, lw_ref, 1, h), go, 1, 1)
        plane = dot(scaled_queries(q_t, lw_ref, 0, h), go, 1, 1)
        mine = first if h < NH // 2 else jnp.logical_not(first)

        def store(far_ref, plane_ref, far=far, plane=plane, h=h):
            for m in range(PLANE):
                for i in range(16):
                    row = m * HD + 8 * i
                    far_ref[16 * (h % 2) + i, m] = far[row : row + 8]
                plane_ref[m, h % 2] = plane[m * HD : (m + 1) * HD]

        pl.when(mine)(functools.partial(store, own_ref, keep_ref))
        pl.when(jnp.logical_not(mine))(functools.partial(store, send_ref, give_ref))


def pair_body(own_ref, gath_ref, out_ref):
    other = 1 - lax.axis_index("core")
    out_ref[...] = own_ref[...] + gath_ref[other]


def join_body(keep_ref, gath_ref, first_ref, second_ref):
    other = 1 - lax.axis_index("core")
    for h in range(NH // 2):
        first_ref[h] = keep_ref[1, h] + gath_ref[other, 1, h]
        second_ref[h] = keep_ref[2, h] + gath_ref[other, 2, h]


def merge_body(piece_ref, back1_ref, back2_ref, keep_ref, gath_ref, mine_ref, send_ref):
    first = lax.axis_index("core") == 0
    zero = jnp.float32(0.0)
    for h in range(NH // 2):
        total = piece_ref[h] + (back1_ref[h] + back2_ref[h])
        mine_ref[h] = total + jnp.where(first, gath_ref[1, 0, h], zero)
        send_ref[h] = total + jnp.where(first, zero, keep_ref[0, h])


def owner_backward_body(in_ref, out_ref):
    grads = []
    for m in range(PLANE):
        rows = []
        for z in range(8):
            total = in_ref[4 * z, m]
            for x in range(1, 4):
                total = total + in_ref[4 * z + x, m]
            rows.append(total)
        grads.append(rows)
    pair2 = grads[1][2] + grads[1][3]
    pair6 = grads[1][6] + grads[1][7]
    four = (grads[2][4] + grads[2][5]) + (grads[2][6] + grads[2][7])
    for z in range(8):
        total = jnp.zeros((8, HD), F32)
        if not z & 1:
            total = total + grads[0][z + 1]
        if not z & 2:
            total = total + (pair6 if z & 4 else pair2)
        if not z & 4:
            total = total + four
        for x in range(4):
            out_ref[4 * z + x] = total


def back_body(
    recv_ref, gain_ref, lw_ref, q_ref, k_ref, v_ref, mixed_ref, att_ref, low_ref, pc_ref,
    nm_ref, gq_ref, gk_ref, gv_ref, gl_ref,
):
    level = level_masks()
    inv_row, coef_row = token_rows(recv_ref)

    def step(h):
        q, k, att = q_ref[h], k_ref[h], att_ref[h]
        go = (inv_row * mixed_ref[h] - att * coef_row).astype(BF16)
        nm_ref[h] = ((att * inv_row).T * gain_ref[h : h + 1, :]).astype(BF16)
        scores = dot(k, q, 1, 1)
        weights = near_weights(lw_ref, level, h)
        mix = dot(v_ref[h], go, 1, 0)
        gv_ref[h] = dot((weights * scores).astype(BF16), go, 1, 1)
        grad_scores = (weights * mix).astype(BF16)
        gk_ref[h] = dot(grad_scores, q, 1, 0)
        product = mix * scores
        rows = []
        for number in range(LOCAL):
            picked = jnp.where(level == number, product, jnp.float32(0.0))
            rows.append(level_scale(number) * jnp.sum(picked, axis=0, keepdims=True))
        q_t = q.astype(F32).T
        far_t = dot(k, grad_scores, 0, 0)
        for part in range(2):
            turned = dot(far_states(pc_ref, h) if part else low_ref[h], go, 1, 0)
            for m in range(PLANE):
                piece = turned[m * HD : (m + 1) * HD]
                number = LOCAL + part * PLANE + m
                far_t = far_t + level_row(lw_ref, number, h) * piece
                rows.append(level_scale(number) * jnp.sum(piece * q_t, axis=0, keepdims=True))
        gq_ref[h] = far_t.T.astype(BF16)
        for number in range(LOCAL + FAR):
            gl_ref[number, h : h + 1, :] = rows[number]

    return step


def final_body(mine_ref, wide_ref, k_ref, v_ref, gk_ref, gv_ref, outk_ref, outv_ref):
    first = lax.axis_index("core") == 0

    def step(h):
        mine = first if h < NH // 2 else jnp.logical_not(first)
        grad_kv = jnp.where(mine, mine_ref[h % 2], wide_ref[h // 2, h % 2]).astype(BF16)
        outk_ref[h] = (gk_ref[h] + dot(v_ref[h], grad_kv, 1, 1)).astype(BF16)
        outv_ref[h] = (gv_ref[h] + dot(k_ref[h], grad_kv, 1, 0)).astype(BF16)

    return step


def swap(value, axes):
    return lax.all_to_all(value, axes, split_axis=0, concat_axis=0, tiled=True)


def both_cores(value):
    return lax.all_gather(value, "core", axis=0, tiled=False)


def shards(queries, key_rows, value_rows, level_weights, norm_gain, grad_normed):
    rates = jnp.transpose(level_weights, (1, 0, 2))
    (kv,) = call(
        key_value_body,
        [(MATRIX, F32)],
        (key_rows, value_rows),
        2**25,
        MIB,
        (0, 1),
        (0,),
        ALONE,
        whole_in=True,
    )
    both = both_cores(kv)
    (pair,) = call(half_body, [(HALF, F32)], (both,), 2**16, MIB)
    owned = swap(pair.reshape(32, 8, HD), ROWS)
    step1 = lax.ppermute(pair, "x", [(0, 1), (1, 0), (2, 3), (3, 2)])
    (twice,) = call(add_body, [(HALF, F32)], (pair, step1), 2**16, MIB)
    (outgoing,) = call(
        owner_forward_body, [(PIECES, F32)], (owned,), 2**17, MIB // 2, after=(twice,)
    )
    arrived = swap(outgoing, ROWS)
    step2 = lax.ppermute(twice, "x", [(0, 3), (1, 2)])
    (wide,) = call(
        collect_body,
        [((2,) + HALF, F32)],
        (step1, step2),
        2**16,
        MIB,
    )
    mixed, low, q_turned = call(
        near_body,
        [((NH, 2, HD, TOK), F32), (STACKED, BF16), (TURNED, BF16)],
        (
            rates, norm_gain, both_cores(wide), both, queries, key_rows, value_rows, grad_normed,
        ),
        2**34,
        4 * MIB,
        tuple(range(8)),
        tuple(range(3)),
        ALONE,
        views={3: (MATRIX, lambda ref: ref.at[0])},
    )
    gathered = both_cores(arrived)
    attended, payload = call(
        attend_body,
        [(TURNED, F32), ((8, 4, HD), F32)],
        (gathered, rates, queries, mixed),
        2**27,
        4 * MIB,
    )
    sums = swap(payload, "heads")
    own, send, keep, give = call(
        grad_body,
        [
            (PIECES, F32),
            (PIECES, F32),
            ((PLANE,) + HALF, F32),
            ((PLANE,) + HALF, F32),
        ],
        (sums, rates, attended, mixed, q_turned),
        2**28,
        6 * MIB,
    )
    (joined,) = call(pair_body, [(PIECES, F32)], (own, both_cores(send)), 2**17, 3 * MIB // 2)
    returned = swap(joined, ROWS)
    given = both_cores(give)
    first, second = call(join_body, [(HALF, F32), (HALF, F32)], (keep, given), 2**17, MIB)
    back2 = lax.ppermute(second, "x", [(3, 0), (2, 1)])
    normed, grad_q, near_k, near_v, grad_rates = call(
        back_body,
        [(TOKENS, BF16), (TOKENS, BF16), (TOKENS, F32), (TOKENS, F32), ((LOCAL + FAR, NH, TOK), F32)],
        (
            sums, norm_gain, rates, queries, key_rows, value_rows, mixed, attended, low, gathered,
        ),
        2**34,
        5 * MIB,
        tuple(range(10)),
        tuple(range(5)),
        ALONE,
        views={6: (TURNED, lambda ref: ref.at[:, 1])},
    )
    returned, back2, near_k = lax.optimization_barrier((returned, back2, near_k))
    (spread,) = call(owner_backward_body, [((32, 8, HD), F32)], (returned,), 2**17, MIB // 2)
    pieces = swap(spread, ROWS).reshape(HALF)
    (onward,) = call(add_odd_body, [(HALF, F32)], (first, back2), 2**16, MIB, after=(spread,))
    back1 = lax.ppermute(onward, "x", [(0, 1), (1, 0), (3, 2)])
    mine, theirs = call(
        merge_body, [(HALF, F32), (HALF, F32)], (pieces, back1, back2, keep, given), 2**16, MIB
    )
    grad_k, grad_v = call(
        final_body,
        [(TOKENS, BF16), (TOKENS, BF16)],
        (mine, both_cores(theirs), key_rows, value_rows, near_k, near_v),
        2**26,
        3 * MIB,
    )
    return normed, grad_q, grad_k, grad_v, jnp.transpose(grad_rates, (1, 0, 2))


def solution(mesh):
    grid = Mesh(mesh.devices.reshape(8, 8, 4, 2), ("heads",) + CTX)
    rows = P("heads", CTX, None)
    rates = P("heads", None, CTX)
    return jax.shard_map(
        shards,
        mesh=grid,
        in_specs=(rows, rows, rows, rates, P("heads", None), rows),
        out_specs=(rows, rows, rows, rows, rates),
        check_vma=False,
    )
```

```python
import functools
import math

import jax
import jax.numpy as jnp
from jax import lax
from jax.experimental import pallas as pl
from jax.experimental.pallas import tpu as pltpu
from jax.sharding import Mesh
from jax.sharding import PartitionSpec as P

EPS = 1e-06
F32 = jnp.float32
BF16 = jnp.bfloat16

NH = 4
TOK = 256
HD = 128
LOCAL = 9
FAR = 6
PLANE = 3
WIDTH = 32 * HD
MIB = 2**20
ALONE = 60

CTX = ("z", "x", "core")
ROWS = ("x", "z")

TOKENS = (NH, TOK, HD)
TURNED = (NH, HD, TOK)
MATRIX = (NH, HD, HD)
HALF = (NH // 2, HD, HD)
STACKED = (NH, PLANE * HD, HD)
PIECES = (32, PLANE, 8, HD)


def level_scale(number):
    return 2.0 ** (-max(number - 1, 0) / 2.0) / math.sqrt(HD)


def dot(a, b, ca, cb):
    return lax.dot_general(a, b, (((ca,), (cb,)), ((), ())), preferred_element_type=F32)


def call(body, outs, operands, flops, moved, far_in=(), far_out=(), limit=16, after=(), views={}, whole_in=False):
    near = pl.BlockSpec(memory_space=pltpu.VMEM)
    far = pl.BlockSpec(memory_space=pltpu.HBM)
    count = len(operands)
    shapes = [views[i][0] if i in views else a.shape for i, a in enumerate(operands)]
    buffers = [pltpu.VMEM(shapes[i], operands[i].dtype) for i in far_in]
    buffers += [pltpu.VMEM(*outs[i]) for i in far_out]

    def split(shape):
        return shape[0] == NH and len(shape) > 2

    parts = [NH if split(shapes[i]) and not whole_in else 1 for i in far_in]
    parts += [NH if split(outs[i][0]) else 1 for i in far_out]
    copies = sum(parts)

    def wrapped(*refs):
        refs = list(refs)
        sems = refs.pop() if copies else None
        del refs[count : count + len(after)]
        scratch = refs[count + len(outs) :]
        used = refs[: count + len(outs)]
        whole, before, behind, last = [], [[] for _ in range(NH)], [[] for _ in range(NH)], []
        sem = 0
        for slot, i in enumerate(far_in):
            held = scratch[slot]
            if i in views:
                used[i] = views[i][1](used[i])
            if parts[slot] == NH:
                for h in range(NH):
                    before[h].append(
                        pltpu.make_async_copy(used[i].at[h], held.at[h], sems.at[sem + h])
                    )
            else:
                whole.append(pltpu.make_async_copy(used[i], held, sems.at[sem]))
            sem += parts[slot]
            used[i] = held
        for slot, i in enumerate(far_out, len(far_in)):
            held = scratch[slot]
            if parts[slot] == NH:
                for h in range(NH):
                    behind[h].append(
                        pltpu.make_async_copy(held.at[h], used[count + i].at[h], sems.at[sem + h])
                    )
            else:
                last.append(pltpu.make_async_copy(held, used[count + i], sems.at[sem]))
            sem += parts[slot]
            used[count + i] = held
        for copy in whole + sum(before, []):
            copy.start()
        for copy in whole:
            copy.wait()
        step = body(*used)
        for h in range(NH):
            for copy in before[h]:
                copy.wait()
            if step is not None:
                step(h)
            for copy in behind[h]:
                copy.start()
        for copy in last:
            copy.start()
        for copy in sum(behind, []) + last:
            copy.wait()

    return pl.pallas_call(
        wrapped,
        out_shape=[jax.ShapeDtypeStruct(s, d) for s, d in outs],
        in_specs=[far if i in far_in else near for i in range(count)]
        + [pl.BlockSpec(memory_space=pl.ANY)] * len(after),
        out_specs=[far if i in far_out else near for i in range(len(outs))],
        scratch_shapes=buffers + ([pltpu.SemaphoreType.DMA((copies,))] if copies else []),
        cost_estimate=pl.CostEstimate(flops=flops, bytes_accessed=moved, transcendentals=0),
        compiler_params=pltpu.CompilerParams(vmem_limit_bytes=int(limit * MIB)),
    )(*operands, *after)


def key_value_body(k_ref, v_ref, kv_ref):
    def step(h):
        kv_ref[h] = dot(k_ref[h], v_ref[h], 0, 0)

    return step


def level_masks():
    s = lax.broadcasted_iota(jnp.int32, (TOK, TOK), 0)
    t = lax.broadcasted_iota(jnp.int32, (TOK, TOK), 1)
    differ = s ^ t
    bucket = jnp.zeros((TOK, TOK), jnp.int32)
    for exponent in range(LOCAL - 1):
        bucket = bucket + (differ >= 2**exponent).astype(jnp.int32)
    return jnp.where(s <= t, bucket, -1)


def level_row(lw_ref, number, h):
    return lw_ref[number, h : h + 1, :] * level_scale(number)


def near_weights(lw_ref, level, h):
    weights = jnp.zeros((TOK, TOK), F32)
    for number in range(LOCAL):
        weights = jnp.where(level == number, level_row(lw_ref, number, h), weights)
    return weights


def scaled_queries(q_t, lw_ref, part, h):
    levels = [LOCAL + part * PLANE + m for m in range(PLANE)]
    return jnp.concatenate([q_t * level_row(lw_ref, n, h) for n in levels], axis=0).astype(BF16)


def near_body(
    lw_ref, gain_ref, wide_ref, both_ref, q_ref, k_ref, v_ref, gn_ref, mixed_ref, st_ref, qt_ref
):
    level = level_masks()
    odd = lax.axis_index("core") == 1

    def step(h):
        q = q_ref[h]
        scores = dot(k_ref[h], q, 1, 1)
        weighted = (near_weights(lw_ref, level, h) * scores).astype(BF16)
        q_t = q.astype(F32).T
        qt_ref[h] = q_t.astype(BF16)
        s0 = jnp.where(odd, both_ref[h], jnp.float32(0.0))
        s1 = wide_ref[h // 2, 0, h % 2]
        s2 = wide_ref[h // 2, 1, h % 2]
        states = jnp.concatenate([s0, s1, s2], axis=0).astype(BF16)
        st_ref[h] = states
        far = dot(states, scaled_queries(q_t, lw_ref, 0, h), 0, 0)
        mixed_ref[h, 0] = dot(v_ref[h], weighted, 0, 0) + far
        mixed_ref[h, 1] = (gain_ref[h : h + 1, :] * gn_ref[h].astype(F32)).T

    return step


def half_body(both_ref, out_ref):
    first = lax.axis_index("core") * (NH // 2)
    for h in range(NH // 2):
        out_ref[h] = both_ref[0, first + h] + both_ref[1, first + h]


def collect_body(step1_ref, step2_ref, out_ref):
    odd = (lax.axis_index("x") & 1) == 1
    for h in range(NH // 2):
        out_ref[0, h] = jnp.where(odd, step1_ref[h], jnp.float32(0.0))
        out_ref[1, h] = step2_ref[h]


def add_body(a_ref, b_ref, out_ref):
    out_ref[...] = a_ref[...] + b_ref[...]


def add_odd_body(a_ref, b_ref, out_ref):
    odd = (lax.axis_index("x") & 1) == 1
    out_ref[...] = jnp.where(odd, a_ref[...], jnp.float32(0.0)) + b_ref[...]


def owner_forward_body(in_ref, out_ref):
    sums = []
    for z in range(8):
        total = in_ref[z]
        for x in range(1, 4):
            total = total + in_ref[8 * x + z]
        sums.append(total)
    nothing = jnp.zeros((8, HD), F32)
    pair0 = sums[0] + sums[1]
    pair2 = sums[4] + sums[5]
    four = pair0 + (sums[2] + sums[3])
    for z in range(8):
        first = sums[z - 1] if z & 1 else nothing
        second = (pair2 if z & 4 else pair0) if z & 2 else nothing
        third = four if z & 4 else nothing
        for x in range(4):
            out_ref[8 * x + z, 0] = first
            out_ref[8 * x + z, 1] = second
            out_ref[8 * x + z, 2] = third


def far_states(pc_ref, h):
    tiles = []
    for m in range(PLANE):
        for i in range(16):
            tiles.append(pc_ref[h // 2, 16 * (h % 2) + i, m])
    return jnp.concatenate(tiles, axis=0).astype(BF16)


def attend_body(pc_ref, lw_ref, q_ref, mixed_ref, att_ref, pay_ref):
    squares = jnp.zeros((HD, TOK), F32)
    inner = jnp.zeros((HD, TOK), F32)
    for h in range(NH):
        states = far_states(pc_ref, h)
        att = mixed_ref[h, 0]
        for m in range(PLANE):
            far = dot(states[m * HD : (m + 1) * HD], q_ref[h], 0, 1)
            att = att + level_row(lw_ref, LOCAL + PLANE + m, h) * far
        att_ref[h] = att
        squares = squares + att * att
        inner = inner + mixed_ref[h, 1] * att
    squares = jnp.sum(squares, axis=0, keepdims=True)
    inner = jnp.sum(inner, axis=0, keepdims=True)
    rows = [squares[:, :HD], squares[:, HD:], inner[:, :HD], inner[:, HD:]]
    tile = jnp.concatenate(rows, axis=0)
    for peer in range(8):
        pay_ref[peer] = tile


def token_rows(recv_ref):
    total = recv_ref[0]
    for peer in range(1, 8):
        total = total + recv_ref[peer]
    inv = lax.rsqrt(total[0:2] / WIDTH + EPS)
    coef = inv * inv * inv * total[2:4] / WIDTH
    inv_row = jnp.concatenate([inv[0:1], inv[1:2]], axis=1)
    coef_row = jnp.concatenate([coef[0:1], coef[1:2]], axis=1)
    return inv_row, coef_row


def grad_body(
    recv_ref, lw_ref, att_ref, mixed_ref, qt_ref, own_ref, send_ref, keep_ref, give_ref
):
    first = lax.axis_index("core") == 0
    inv_row, coef_row = token_rows(recv_ref)
    for h in range(NH):
        go = (inv_row * mixed_ref[h, 1] - att_ref[h] * coef_row).astype(BF16)
        q_t = qt_ref[h].astype(F32)
        far = dot(scaled_queries(q_t, lw_ref, 1, h), go, 1, 1)
        plane = dot(scaled_queries(q_t, lw_ref, 0, h), go, 1, 1)
        mine = first if h < NH // 2 else jnp.logical_not(first)

        def store(far_ref, plane_ref, far=far, plane=plane, h=h):
            for m in range(PLANE):
                for i in range(16):
                    row = m * HD + 8 * i
                    far_ref[16 * (h % 2) + i, m] = far[row : row + 8]
                plane_ref[m, h % 2] = plane[m * HD : (m + 1) * HD]

        pl.when(mine)(functools.partial(store, own_ref, keep_ref))
        pl.when(jnp.logical_not(mine))(functools.partial(store, send_ref, give_ref))


def pair_body(own_ref, gath_ref, out_ref):
    other = 1 - lax.axis_index("core")
    out_ref[...] = own_ref[...] + gath_ref[other]


def join_body(keep_ref, gath_ref, first_ref, second_ref):
    other = 1 - lax.axis_index("core")
    for h in range(NH // 2):
        first_ref[h] = keep_ref[1, h] + gath_ref[other, 1, h]
        second_ref[h] = keep_ref[2, h] + gath_ref[other, 2, h]


def merge_body(piece_ref, back1_ref, back2_ref, keep_ref, gath_ref, mine_ref, send_ref):
    first = lax.axis_index("core") == 0
    zero = jnp.float32(0.0)
    for h in range(NH // 2):
        total = piece_ref[h] + (back1_ref[h] + back2_ref[h])
        mine_ref[h] = total + jnp.where(first, gath_ref[1, 0, h], zero)
        send_ref[h] = total + jnp.where(first, zero, keep_ref[0, h])


def owner_backward_body(in_ref, out_ref):
    grads = []
    for m in range(PLANE):
        rows = []
        for z in range(8):
            total = in_ref[z, m]
            for x in range(1, 4):
                total = total + in_ref[8 * x + z, m]
            rows.append(total)
        grads.append(rows)
    pair2 = grads[1][2] + grads[1][3]
    pair6 = grads[1][6] + grads[1][7]
    four = (grads[2][4] + grads[2][5]) + (grads[2][6] + grads[2][7])
    for z in range(8):
        total = jnp.zeros((8, HD), F32)
        if not z & 1:
            total = total + grads[0][z + 1]
        if not z & 2:
            total = total + (pair6 if z & 4 else pair2)
        if not z & 4:
            total = total + four
        for x in range(4):
            out_ref[8 * x + z] = total


def back_body(
    recv_ref, gain_ref, lw_ref, q_ref, k_ref, v_ref, mixed_ref, att_ref, low_ref, pc_ref,
    nm_ref, gq_ref, gk_ref, gv_ref, gl_ref,
):
    level = level_masks()
    inv_row, coef_row = token_rows(recv_ref)

    def step(h):
        q, k, att = q_ref[h], k_ref[h], att_ref[h]
        go = (inv_row * mixed_ref[h] - att * coef_row).astype(BF16)
        nm_ref[h] = ((att * inv_row).T * gain_ref[h : h + 1, :]).astype(BF16)
        scores = dot(k, q, 1, 1)
        weights = near_weights(lw_ref, level, h)
        mix = dot(v_ref[h], go, 1, 0)
        gv_ref[h] = dot((weights * scores).astype(BF16), go, 1, 1)
        grad_scores = (weights * mix).astype(BF16)
        gk_ref[h] = dot(grad_scores, q, 1, 0)
        product = mix * scores
        rows = []
        for number in range(LOCAL):
            picked = jnp.where(level == number, product, jnp.float32(0.0))
            rows.append(level_scale(number) * jnp.sum(picked, axis=0, keepdims=True))
        q_t = q.astype(F32).T
        far_t = dot(k, grad_scores, 0, 0)
        for part in range(2):
            turned = dot(far_states(pc_ref, h) if part else low_ref[h], go, 1, 0)
            for m in range(PLANE):
                piece = turned[m * HD : (m + 1) * HD]
                number = LOCAL + part * PLANE + m
                far_t = far_t + level_row(lw_ref, number, h) * piece
                rows.append(level_scale(number) * jnp.sum(piece * q_t, axis=0, keepdims=True))
        gq_ref[h] = far_t.T.astype(BF16)
        for number in range(LOCAL + FAR):
            gl_ref[number, h : h + 1, :] = rows[number]

    return step


def final_body(mine_ref, wide_ref, k_ref, v_ref, gk_ref, gv_ref, outk_ref, outv_ref):
    first = lax.axis_index("core") == 0

    def step(h):
        mine = first if h < NH // 2 else jnp.logical_not(first)
        grad_kv = jnp.where(mine, mine_ref[h % 2], wide_ref[h // 2, h % 2]).astype(BF16)
        outk_ref[h] = (gk_ref[h] + dot(v_ref[h], grad_kv, 1, 1)).astype(BF16)
        outv_ref[h] = (gv_ref[h] + dot(k_ref[h], grad_kv, 1, 0)).astype(BF16)

    return step


def swap(value, axes):
    return lax.all_to_all(value, axes, split_axis=0, concat_axis=0, tiled=True)


def both_cores(value):
    return lax.all_gather(value, "core", axis=0, tiled=False)


def shards(queries, key_rows, value_rows, level_weights, norm_gain, grad_normed):
    rates = jnp.transpose(level_weights, (1, 0, 2))
    (kv,) = call(
        key_value_body,
        [(MATRIX, F32)],
        (key_rows, value_rows),
        2**25,
        MIB,
        (0, 1),
        (0,),
        ALONE,
        whole_in=True,
    )
    both = both_cores(kv)
    (pair,) = call(half_body, [(HALF, F32)], (both,), 2**16, MIB)
    owned = swap(pair.reshape(32, 8, HD), ROWS)
    step1 = lax.ppermute(pair, "x", [(0, 1), (1, 0), (2, 3), (3, 2)])
    (twice,) = call(add_body, [(HALF, F32)], (pair, step1), 2**16, MIB)
    (outgoing,) = call(
        owner_forward_body, [(PIECES, F32)], (owned,), 2**17, MIB // 2, after=(twice,)
    )
    arrived = swap(outgoing, ROWS)
    step2 = lax.ppermute(twice, "x", [(0, 3), (1, 2)])
    (wide,) = call(
        collect_body,
        [((2,) + HALF, F32)],
        (step1, step2),
        2**16,
        MIB,
    )
    mixed, low, q_turned = call(
        near_body,
        [((NH, 2, HD, TOK), F32), (STACKED, BF16), (TURNED, BF16)],
        (
            rates, norm_gain, both_cores(wide), both, queries, key_rows, value_rows, grad_normed,
        ),
        2**34,
        4 * MIB,
        tuple(range(8)),
        tuple(range(3)),
        ALONE,
        whole_in=True,
        views={3: (MATRIX, lambda ref: ref.at[0])},
    )
    gathered = both_cores(arrived)
    attended, payload = call(
        attend_body,
        [(TURNED, F32), ((8, 4, HD), F32)],
        (gathered, rates, queries, mixed),
        2**27,
        4 * MIB,
    )
    sums = swap(payload, "heads")
    own, send, keep, give = call(
        grad_body,
        [
            (PIECES, F32),
            (PIECES, F32),
            ((PLANE,) + HALF, F32),
            ((PLANE,) + HALF, F32),
        ],
        (sums, rates, attended, mixed, q_turned),
        2**28,
        6 * MIB,
    )
    (joined,) = call(pair_body, [(PIECES, F32)], (own, both_cores(send)), 2**17, 3 * MIB // 2)
    returned = swap(joined, ROWS)
    given = both_cores(give)
    first, second = call(join_body, [(HALF, F32), (HALF, F32)], (keep, given), 2**17, MIB)
    back2 = lax.ppermute(second, "x", [(3, 0), (2, 1)])
    normed, grad_q, near_k, near_v, grad_rates = call(
        back_body,
        [(TOKENS, BF16), (TOKENS, BF16), (TOKENS, F32), (TOKENS, F32), ((LOCAL + FAR, NH, TOK), F32)],
        (
            sums, norm_gain, rates, queries, key_rows, value_rows, mixed, attended, low, gathered,
        ),
        2**34,
        5 * MIB,
        tuple(range(10)),
        tuple(range(5)),
        ALONE,
        views={6: (TURNED, lambda ref: ref.at[:, 1])},
    )
    returned, back2, near_k = lax.optimization_barrier((returned, back2, near_k))
    (spread,) = call(owner_backward_body, [((32, 8, HD), F32)], (returned,), 2**17, MIB // 2)
    pieces = swap(spread, ROWS).reshape(HALF)
    (onward,) = call(add_odd_body, [(HALF, F32)], (first, back2), 2**16, MIB, after=(spread,))
    back1 = lax.ppermute(onward, "x", [(0, 1), (1, 0), (3, 2)])
    mine, theirs = call(
        merge_body, [(HALF, F32), (HALF, F32)], (pieces, back1, back2, keep, given), 2**16, MIB
    )
    grad_k, grad_v = call(
        final_body,
        [(TOKENS, BF16), (TOKENS, BF16)],
        (mine, both_cores(theirs), key_rows, value_rows, near_k, near_v),
        2**26,
        3 * MIB,
    )
    return normed, grad_q, grad_k, grad_v, jnp.transpose(grad_rates, (1, 0, 2))


def solution(mesh):
    grid = Mesh(mesh.devices.reshape(8, 8, 4, 2), ("heads",) + CTX)
    rows = P("heads", CTX, None)
    rates = P("heads", None, CTX)
    return jax.shard_map(
        shards,
        mesh=grid,
        in_specs=(rows, rows, rows, rates, P("heads", None), rows),
        out_specs=(rows, rows, rows, rows, rates),
        check_vma=False,
    )
```
